128 devices in a mesh: dp: 4 (over y), expert: 32 (over x, z, core).
Axes of the slice: x: 4, y: 4, z: 4, core: 2. Of those that a mesh axis runs over, the one named last changes fastest.
Arguments:
- tokens: bfloat16 [16384, 3584], P(('dp', 'expert')), may hold values from -6 to 6
- gate_probs: float32 [16384, 8], P(('dp', 'expert')), may hold values from 0.1 to 1
- expert_ids: int32 [16384, 8], P(('dp', 'expert')), may hold values from 0 to 255, all different within a row; in each aligned block of 128 rows (0 to 127, 128 to 255, ...) at most 6 rows name the same one
- cotangent: bfloat16 [16384, 3584], P(('dp', 'expert')), may hold values from -6 to 6
- w_gate: bfloat16 [32, 3584, 2048], P('expert', None, 'dp'), may hold values from -0.09375 to 0.09375
- w_up: bfloat16 [32, 3584, 2048], P('expert', None, 'dp'), may hold values from -0.09375 to 0.09375
- w_down: bfloat16 [32, 2048, 3584], P('expert', 'dp'), may hold values from -0.125 to 0.125
Outputs:
- layer_out: bfloat16 [16384, 3584], P(('dp', 'expert'))
- grad_tokens: bfloat16 [16384, 3584], P(('dp', 'expert'))
- grad_probs: float32 [16384, 8], P(('dp', 'expert'))
- grad_gate: bfloat16 [32, 3584, 2048], P('expert', None, 'dp')
- grad_up: bfloat16 [32, 3584, 2048], P('expert', None, 'dp')
- grad_down: bfloat16 [32, 2048, 3584], P('expert', 'dp')
The draws below stay inside these ranges and needn't reach their ends.
Inputs may be any that keep to these rules, and one draw needn't show every extreme that they name: `expert_ids`: each token names 8 distinct ids. Among the 128 tokens of one device no id is named by more than 6 of them, a bound that some block reaches. Only ids below 32 belong to the window.
All inputs are finite; a program needn't handle non-finite values.
Results may differ from the reference program's by a relative error of at most 0.012.
Values may be sent and summed in bfloat16 or wider, within the bound.
A program may use at most 192 MiB of HBM per device.

```python
import math
import jax
import jax.numpy as jnp
import numpy as np
from jax import lax

D = 3584
FF_DEV = 512
TOP = 8
TOK_DEV = 128
FF = 2048
EXPERTS = 32
ALL_EXPERTS = 256
CAP = 6
TOKENS = 16384
N_DP = 4
DEVICES = 128


def level_of(stream_key, shape, split, smallest, largest):
    def one(position, parts):
        draws = jax.random.uniform(jax.random.fold_in(jax.random.fold_in(stream_key, 6), position), (parts,), jnp.float32, smallest / len(split), largest / len(split))
        return jnp.repeat(jnp.exp(draws), shape[position] // parts).reshape((-1,) + (1,) * (len(shape) - position - 1))

    level = one(*split[0])
    for cut in split[1:]:
        level = level * one(*cut)
    return level


def assign_block(key, own, number, rows, number_of, top, limit, slope):
    order = jax.random.permutation(key, number_of)
    packed, ordinary = shares(number_of, rows * top, limit, slope, True), shares(number_of, rows * top, limit, slope, False)
    places = jnp.arange(number_of)

    def named(lengths, rotation):
        used = int((lengths > 0).sum())
        fixed = max(1, used // 4)
        shifted = fixed + (places - fixed + rotation * (used - fixed)) % max(1, number_of - fixed)
        return jnp.zeros((number_of,), jnp.int32).at[order[jnp.where(places < fixed, places, shifted)]].set(jnp.asarray(lengths, jnp.int32))

    lengths = jnp.where(number % 4 == 0, named(packed, number // 4), named(ordinary, number - number // 4 - 1))
    mixed = jax.random.permutation(jax.random.fold_in(own, 3), number_of)
    source_of, taker = mixed[0:number_of // 2 * 2:2], mixed[1:number_of // 2 * 2:2]
    slack = jnp.minimum(lengths[source_of] - 1, limit - lengths[taker]) // 2
    slack = jnp.where((source_of == order[0]) | (taker == order[0]) | (lengths[taker] == 0), 0, jnp.maximum(slack, 0))
    shifted = jax.random.randint(jax.random.fold_in(own, 4), (number_of // 2,), 0, 1 << 20) % (slack + 1)
    lengths = lengths.at[source_of].add(-shifted).at[taker].add(shifted)
    items = jnp.searchsorted(jnp.cumsum(lengths), jnp.arange(rows * top), side="right").astype(jnp.int32)
    table = items.reshape(top, rows).T
    table = table[jax.random.permutation(jax.random.fold_in(own, 1), rows)]
    rotation = jax.random.randint(jax.random.fold_in(own, 2), (rows, 1), 0, top)
    return jnp.take_along_axis(table, (jnp.arange(top)[None, :] + rotation) % top, axis=1)


def shares(count, total, most, skew, full):
    weights = [(1 << 20) // math.isqrt(rank ** skew) + 1 for rank in range(1, count + 1)]
    largest = most if full else min(most, max(-(-total // count), total * weights[0] // sum(weights)))
    least = 1 if total - largest >= count - 1 else 0
    counts, surplus = [largest] + [least] * (count - 1), total - largest - least * (count - 1)
    while surplus > 0:
        movable = [i for i in range(1, count) if counts[i] < largest] or [i for i in range(1, count) if counts[i] < most]
        mass, remaining = sum([weights[i] for i in movable]), surplus
        for i in movable:
            more = min(most - counts[i], max(1, remaining * weights[i] // mass), surplus)
            counts[i] = counts[i] + more
            surplus = surplus - more
    return np.array(counts)


def noise(stream_key, dims, deviation, bound, shards=(), held_as=jnp.bfloat16):
    drawn = deviation * jax.random.normal(stream_key, dims, jnp.float32)
    if shards:
        drawn = drawn * level_of(stream_key, dims, shards, -0.22, 0.18)
    return jnp.clip(drawn, -bound, bound).astype(held_as)


def setup_inputs(seed: int = 0) -> dict:
    arg_keys = jax.random.split(jax.random.key(seed), 8)
    tokens = noise(arg_keys[0], (TOKENS, D), 1.0, 6.0, ((0, 128),))
    gate_probs = jnp.clip(0.1 + 0.9 * jax.random.uniform(arg_keys[1], (TOKENS, TOP), jnp.float32) ** level_of(arg_keys[1], (TOKENS, TOP), ((0, 128),), -0.2, 0.2), 0.1, 1.0)
    expert_ids_keys = jax.random.split(jax.random.fold_in(arg_keys[2], 1), TOKENS // TOK_DEV)
    expert_ids_turns = jax.random.permutation(jax.random.fold_in(arg_keys[2], 3), TOKENS // TOK_DEV)
    expert_ids = jax.vmap(lambda own, number: assign_block(jax.random.fold_in(arg_keys[2], 2), own, number, TOK_DEV, ALL_EXPERTS, TOP, CAP, 2))(expert_ids_keys, expert_ids_turns).reshape((TOKENS, TOP))
    cotangent = noise(arg_keys[3], (TOKENS, D), 1.0, 6.0, ((0, 128),))
    w_gate = noise(arg_keys[4], (EXPERTS, D, FF), D ** -0.5, 0.09375, ((0, 32), (2, 4)))
    w_up = noise(arg_keys[5], (EXPERTS, D, FF), D ** -0.5, 0.09375, ((0, 32), (2, 4)))
    w_down = noise(arg_keys[6], (EXPERTS, FF, D), FF ** -0.5, 0.125, ((0, 32), (1, 4)))
    return {"tokens": tokens, "gate_probs": gate_probs, "expert_ids": expert_ids, "cotangent": cotangent, "w_gate": w_gate, "w_up": w_up, "w_down": w_down}


def device_table(dev_ids):
    flat_ids = dev_ids.reshape(-1).astype(jnp.int32)
    matches = (flat_ids[:, None] == jnp.arange(EXPERTS, dtype=jnp.int32)[None, :]).astype(jnp.int32)
    earlier = jnp.cumsum(matches, axis=0) - matches
    slot_pos = jnp.sum(earlier * matches, axis=1).astype(jnp.int32)
    target = jnp.where(flat_ids < EXPERTS, flat_ids * CAP + slot_pos, EXPERTS * CAP).astype(jnp.int32)
    flat_index = jnp.arange(TOK_DEV * TOP, dtype=jnp.int32)
    blank_table = jnp.full((EXPERTS * CAP,), TOK_DEV * TOP, jnp.int32)
    return blank_table.at[target].set(flat_index, mode="drop")


def reference(tokens, gate_probs, expert_ids, cotangent, w_gate, w_up, w_down):
    dev_ids = expert_ids.reshape(DEVICES, TOK_DEV * TOP)
    local_slots = jax.vmap(device_table)(dev_ids)
    offsets = (jnp.arange(DEVICES, dtype=jnp.int32) * (TOK_DEV * TOP))[:, None]
    global_slots = jnp.where(local_slots < TOK_DEV * TOP, local_slots + offsets, TOKENS * TOP).astype(jnp.int32)
    by_expert = jnp.transpose(global_slots.reshape(DEVICES, EXPERTS, CAP), (1, 0, 2)).reshape(EXPERTS, DEVICES * CAP)
    zero_row = jnp.zeros((1, D), tokens.dtype)
    padded_x = jnp.concatenate([tokens, zero_row], 0)
    padded_dy = jnp.concatenate([cotangent, zero_row], 0)
    padded_p = jnp.concatenate([gate_probs.reshape(-1), jnp.zeros((1,), gate_probs.dtype)], 0)
    row_count = DEVICES * CAP

    def expert_step(running, inputs):
        out_acc, dx_acc, score_acc = running
        gate_w, up_w, down_w, flat_slots = inputs
        token_of = (flat_slots // TOP).astype(jnp.int32)
        rows_x = padded_x[token_of]
        rows_dy = padded_dy[token_of]
        prob_rows = padded_p[flat_slots]
        rows_c = (prob_rows[:, None] * rows_dy.astype(jnp.float32)).astype(jnp.bfloat16)
        gate_pre = jnp.dot(rows_x, gate_w, preferred_element_type=jnp.float32)
        up_pre = jnp.dot(rows_x, up_w, preferred_element_type=jnp.float32)
        sigmoid_g = jax.nn.sigmoid(gate_pre)
        activated = gate_pre * sigmoid_g
        hidden = (activated * up_pre).astype(jnp.bfloat16)
        grad_hidden = jnp.dot(rows_c, down_w.T, preferred_element_type=jnp.float32)
        grad_upin = (grad_hidden * activated).astype(jnp.bfloat16)
        grad_gatein = (grad_hidden * up_pre * sigmoid_g * (1.0 + gate_pre * (1.0 - sigmoid_g))).astype(jnp.bfloat16)
        expert_out = jnp.zeros((row_count, D), jnp.float32)
        dx_rows = jnp.zeros((row_count, D), jnp.float32)
        for quarter in range(N_DP):
            lower = quarter * FF_DEV
            upper = lower + FF_DEV
            part_out = jnp.dot(hidden[:, lower:upper], down_w[lower:upper, :], preferred_element_type=jnp.float32)
            expert_out = expert_out + part_out.astype(jnp.bfloat16).astype(jnp.float32)
            part_dx = jnp.dot(grad_gatein[:, lower:upper], gate_w[:, lower:upper].T, preferred_element_type=jnp.float32)
            part_dx = part_dx + jnp.dot(grad_upin[:, lower:upper], up_w[:, lower:upper].T, preferred_element_type=jnp.float32)
            dx_rows = dx_rows + part_dx.astype(jnp.bfloat16).astype(jnp.float32)
        out_acc = out_acc.at[token_of].add(prob_rows[:, None] * expert_out)
        dx_acc = dx_acc.at[token_of].add(dx_rows)
        score_rows = jnp.sum(rows_dy.astype(jnp.float32) * expert_out, axis=1)
        score_acc = score_acc.at[flat_slots].set(score_rows)
        new_gate = jnp.dot(rows_x.T, grad_gatein, preferred_element_type=jnp.float32).astype(jnp.bfloat16)
        new_up = jnp.dot(rows_x.T, grad_upin, preferred_element_type=jnp.float32).astype(jnp.bfloat16)
        new_down = jnp.dot(hidden.T, rows_c, preferred_element_type=jnp.float32).astype(jnp.bfloat16)
        return (out_acc, dx_acc, score_acc), (new_gate, new_up, new_down)

    start = (jnp.zeros((TOKENS + 1, D), jnp.float32), jnp.zeros((TOKENS + 1, D), jnp.float32), jnp.zeros((TOKENS * TOP + 1,), jnp.float32))
    finals, grads = lax.scan(expert_step, start, (w_gate, w_up, w_down, by_expert))
    out_acc, dx_acc, score_acc = finals
    layer_out = out_acc[:TOKENS].astype(jnp.bfloat16)
    grad_tokens = dx_acc[:TOKENS].astype(jnp.bfloat16)
    grad_probs = score_acc[:TOKENS * TOP].reshape(TOKENS, TOP)
    return (layer_out, grad_tokens, grad_probs, grads[0], grads[1], grads[2])
```

```python
import jax
import jax.numpy as jnp
from jax import lax
from jax.experimental import pallas as pl
from jax.experimental.pallas import tpu as pltpu
from jax.sharding import PartitionSpec as P

MESH = pl.DeviceIdType.MESH
F32 = jnp.float32
BF16 = jnp.bfloat16

D = 3584
FF = 512
TOK = 128
TOP = 8
CAP = 6
NE = 32
NY = 4
NC = 7
CW = D // NC
BLK = 16
PR = NE * BLK
SR = NE * CAP
ROWS = NY * SR
A0 = NC * PR
R0 = 9 * PR


def mo(v, m):
    return pl.multiple_of(v, m)


def nn(a, b):
    return lax.dot_general(a, b, (((1,), (0,)), ((), ())), preferred_element_type=F32)


def nt(a, b):
    return lax.dot_general(a, b, (((1,), (1,)), ((), ())), preferred_element_type=F32)


def tn(a, b):
    return lax.dot_general(a, b, (((0,), (0,)), ((), ())), preferred_element_type=F32)


def kernel(
    tok, probs, ids, cot, wg_hbm, wu_hbm, wd_hbm,
    lo_out, gt_out, gp_out, gg_hbm, gu_hbm, gd_hbm,
    sa, gath, wg, wu, wd, accg, accu, acch, hid, ggi, gui,
    relay, vrec, back, stg, gsel, psel, wout, pack, zacc,
    wsem, asend, arecv, ysend, yrecv, rsend, rrecv, bsend, brecv, gsem,
):
    y = lax.axis_index("dp")
    e = lax.axis_index("expert")
    right, left, across = lax.rem(y + 1, NY), lax.rem(y + 3, NY), lax.rem(y + 2, NY)
    ex, ez, ec = e // 8, lax.rem(e // 2, 4), lax.rem(e, 2)

    def peer(j):
        jx, jz, jc = j // 8, lax.rem(j // 2, 4), lax.rem(j, 2)
        return lax.rem(ex + jx, 4) * 8 + lax.rem(ez + jz, 4) * 2 + lax.rem(ec + jc, 2)

    barrier = pltpu.get_barrier_semaphore()

    def greet(j, carry):
        pl.semaphore_signal(barrier, inc=1, device_id=(y, peer(j)), device_id_type=MESH)
        return carry

    lax.fori_loop(1, NE, greet, 0)
    for side in (right, left):
        pl.semaphore_signal(barrier, inc=1, device_id=(side, e), device_id_type=MESH)

    def weight_copies(n):
        cols = pl.ds(mo(n * CW, CW), CW)
        return (
            pltpu.make_async_copy(wg_hbm.at[cols], wg.at[n], wsem.at[0, n]),
            pltpu.make_async_copy(wu_hbm.at[cols], wu.at[n], wsem.at[1, n]),
            pltpu.make_async_copy(wd_hbm.at[:, cols], wd.at[n], wsem.at[2, n]),
        )

    def start_weights(n, carry):
        for c in weight_copies(n):
            c.start()
        return carry

    lax.fori_loop(0, NC, start_weights, 0)

    lane = lax.broadcasted_iota(jnp.int32, (TOK, TOK), 1)
    sub = lax.broadcasted_iota(jnp.int32, (TOK, TOK), 0)
    named = jnp.zeros((TOK, TOK), F32)
    weight = jnp.zeros((TOK, TOK), F32)
    for k in range(TOP):
        hit = ids[:, k : k + 1] == lane
        named = named + jnp.where(hit, 1.0, 0.0)
        weight = weight + jnp.where(hit, probs[:, k : k + 1], 0.0)
    before = jnp.where(lane < sub, 1.0, 0.0).astype(BF16)
    rank = nn(before, named.astype(BF16))
    code = jnp.where(named > 0.5, rank, 255.0).T[:NE]
    code = jnp.broadcast_to(code[:, None, :], (NE, BLK, TOK)).reshape(PR, TOK)
    weight = jnp.broadcast_to(weight.T[:NE][:, None, :], (NE, BLK, TOK)).reshape(PR, TOK)
    place = lax.rem(lax.broadcasted_iota(jnp.int32, (PR, TOK), 0), BLK)
    slot = place.astype(F32)
    sel_x = jnp.where((place < CAP) & (code == slot), 1.0, 0.0)
    sel_c = jnp.where((place >= CAP) & (place < 2 * CAP) & (code == slot - CAP), 1.0, 0.0)
    gsel[0] = sel_x.astype(BF16)
    gsel[1] = sel_c.astype(BF16)
    psel[...] = jnp.broadcast_to(jnp.sum(sel_c * weight, axis=1, keepdims=True), (PR, TOK))
    by_token = (sel_x * weight).T
    high = by_token.astype(BF16)
    wout[0] = high
    wout[1] = (by_token - high.astype(F32)).astype(BF16)
    wout[2] = sel_c.T.astype(BF16)
    wout[3] = sel_x.T.astype(BF16)
    r_i = lax.broadcasted_iota(jnp.int32, (2 * SR, PR), 0)
    q_i = lax.broadcasted_iota(jnp.int32, (2 * SR, PR), 1)
    kind = jnp.where(r_i >= SR, 1, 0)
    r_i = r_i - kind * SR
    src = r_i // CAP
    pack[...] = jnp.where(q_i == src * BLK + kind * CAP + (r_i - src * CAP), 1.0, 0.0).astype(BF16)
    zacc[...] = jnp.zeros((TOK, PR), F32)

    pl.semaphore_wait(barrier, NE + 1)

    def plane_out(n):
        cols = pl.ds(mo(n * CW, CW), CW)
        rows = nn(gsel[0], tok[:, cols])
        crow = nn(gsel[1], cot[:, cols])
        p = psel[:, 0:1]
        base = mo(n * PR, PR)
        sa[pl.ds(base, PR), :] = (rows + p * crow).astype(BF16)
        sa[pl.ds(mo(A0 + n * PR + e * BLK, BLK), BLK), :] = sa[pl.ds(mo(base + e * BLK, BLK), BLK), :]

        def send(j, carry):
            t = peer(j)
            pltpu.make_async_remote_copy(
                sa.at[pl.ds(mo(n * PR + t * BLK, BLK), BLK)],
                sa.at[pl.ds(mo(A0 + n * PR + e * BLK, BLK), BLK)],
                asend.at[n], arecv.at[n], device_id=(y, t), device_id_type=MESH,
            ).start()
            return carry

        lax.fori_loop(1, NE, send, 0)

    def wait_plane(sem):
        blocks = sa.at[pl.ds(0, PR - BLK)]
        pltpu.make_async_copy(blocks, blocks, sem).wait()

    def own_copy(n, kind, d):
        ref = gath.at[n, kind, y]
        return pltpu.make_async_remote_copy(
            ref, ref, ysend.at[d, kind, n], yrecv.at[d, kind, n],
            device_id=((right, left)[d], e), device_id_type=MESH,
        )

    def pass_copy(n, d):
        ref = gath.at[n, d, (left, right)[d]]
        return pltpu.make_async_remote_copy(
            ref, ref, ysend.at[d, 2, n], yrecv.at[d, 2, n],
            device_id=((right, left)[d], e), device_id_type=MESH,
        )

    plane_out(0)
    plane_out(1)
    accg[...] = jnp.zeros((ROWS, FF), F32)
    accu[...] = jnp.zeros((ROWS, FF), F32)
    acch[...] = jnp.zeros((ROWS, FF), F32)

    def gather_step(i, carry):
        @pl.when(i + 2 < NC)
        def _():
            plane_out(i + 2)

        @pl.when(i < NC)
        def _():
            wait_plane(arecv.at[i])
            both = nn(pack[...], sa[pl.ds(mo(A0 + i * PR, PR), PR), :]).astype(BF16)
            gath[i, 0, y] = both[:SR]
            gath[i, 1, y] = both[SR:]
            for kind in range(2):
                for d in range(2):
                    own_copy(i, kind, d).start()

        @pl.when((i >= 1) & (i <= NC))
        def _():
            n = i - 1
            for d in range(2):
                own_copy(n, d, d).wait_recv()
                pass_copy(n, d).start()
            for d in range(2):
                own_copy(n, 1 - d, d).wait_recv()

        @pl.when(i >= 2)
        def _():
            n = i - 2
            for d in range(2):
                pass_copy(n, d).wait_recv()
            for c in weight_copies(n):
                c.wait()

            def half(h, carry2):
                rows = pl.ds(mo(h * 2 * SR, 2 * SR), 2 * SR)
                xr = gath[n, 0, pl.ds(2 * h, 2)].reshape(2 * SR, CW)
                cr = gath[n, 1, pl.ds(2 * h, 2)].reshape(2 * SR, CW)
                accg[rows, :] += nn(xr, wg[n])
                accu[rows, :] += nn(xr, wu[n])
                acch[rows, :] += nt(cr, wd[n])
                return carry2

            lax.fori_loop(0, 2, half, 0)

        return carry

    lax.fori_loop(0, NC + 2, gather_step, 0)

    def activate(i, carry):
        rows = pl.ds(mo(i * 32, 32), 32)
        g, u, h = accg[rows, :], accu[rows, :], acch[rows, :]
        s = jax.nn.sigmoid(g)
        act = g * s
        hid[rows, :] = (act * u).astype(BF16)
        gui[rows, :] = (h * act).astype(BF16)
        ggi[rows, :] = (h * u * s * (1.0 + g * (1.0 - s))).astype(BF16)
        return carry

    lax.fori_loop(0, ROWS // 32, activate, 0)

    def drain(n, carry):
        wait_plane(asend.at[n])
        for d in range(2):
            for kind in range(2):
                own_copy(n, kind, d).wait_send()
            pass_copy(n, d).wait_send()
        return carry

    lax.fori_loop(0, NC, drain, 0)

    def part(m, kind, b):
        return pl.ds(mo(lax.rem(m, 3) * (2 * ROWS) + kind * ROWS + b * SR, SR), SR)

    def relay_copy(m, d):
        return pltpu.make_async_remote_copy(
            sa.at[part(m, d, across)], relay.at[m, d], rsend.at[d, 2, m], rrecv.at[d, 2, m],
            device_id=((right, left)[d], e), device_id_type=MESH,
        )

    def final_copy(m, kind, d):
        return pltpu.make_async_remote_copy(
            sa.at[part(m, kind, (right, left)[d])], vrec.at[m, d, kind],
            rsend.at[d, kind, m], rrecv.at[d, kind, m],
            device_id=((right, left)[d], e), device_id_type=MESH,
        )

    def sent(m):
        for d in range(2):
            relay_copy(m, d).wait_send()
            for kind in range(2):
                final_copy(m, kind, d).wait_send()

    def grad_copies(m):
        cols = pl.ds(mo(m * CW, CW), CW)
        b = lax.rem(m, 2)
        return (
            pltpu.make_async_copy(stg.at[b, 0], gg_hbm.at[cols], gsem.at[0, m]),
            pltpu.make_async_copy(stg.at[b, 1], gu_hbm.at[cols], gsem.at[1, m]),
            pltpu.make_async_copy(stg.at[b, 2], gd_hbm.at[:, cols], gsem.at[2, m]),
        )

    def back_slot(m):
        return R0 + lax.rem(m, 3) * PR

    def scatter_step(i, carry):
        @pl.when(i < NC)
        def _():
            m = i

            @pl.when(m >= 3)
            def _():
                sent(m - 3)

            def half(h, carry2):
                rows = pl.ds(mo(h * 2 * SR, 2 * SR), 2 * SR)
                base = lax.rem(m, 3) * (2 * ROWS) + h * 2 * SR
                sa[pl.ds(mo(base, SR), 2 * SR), :] = nn(hid[rows, :], wd[m]).astype(BF16)
                dx = nt(ggi[rows, :], wg[m]) + nt(gui[rows, :], wu[m])
                sa[pl.ds(mo(base + ROWS, SR), 2 * SR), :] = dx.astype(BF16)
                return carry2

            lax.fori_loop(0, 2, half, 0)
            for d in range(2):
                relay_copy(m, d).start()
            for d in range(2):
                final_copy(m, 1 - d, d).start()

        @pl.when((i >= 1) & (i <= NC))
        def _():
            m = i - 1
            for d in range(2):
                relay_copy(m, d).wait_recv()
                rows = part(m, d, (right, left)[d])
                sa[rows, :] = (sa[rows, :].astype(F32) + relay[m, d].astype(F32)).astype(BF16)
                final_copy(m, d, d).start()

        @pl.when((i >= 2) & (i <= NC + 1))
        def _():
            m = i - 2
            for d in range(2):
                for kind in range(2):
                    final_copy(m, kind, d).wait_recv()

            @pl.when(m >= 3)
            def _():
                wait_plane(bsend.at[m - 3])

            total = []
            for kind in range(2):
                own = sa[part(m, kind, y), :].astype(F32)
                total.append((own + vrec[m, 0, kind].astype(F32) + vrec[m, 1, kind].astype(F32)).astype(BF16))
            base = back_slot(m)
            spread = tn(pack[:SR, :], total[0]) + tn(pack[SR:, :], total[1])
            sa[pl.ds(mo(base, PR), PR), :] = spread.astype(BF16)
            back[m, pl.ds(mo(e * BLK, BLK), BLK), :] = sa[pl.ds(mo(base + e * BLK, BLK), BLK), :]

            def send(j, carry2):
                t = peer(j)
                pltpu.make_async_remote_copy(
                    sa.at[pl.ds(mo(base + t * BLK, BLK), BLK)],
                    back.at[m, pl.ds(mo(e * BLK, BLK), BLK)],
                    bsend.at[m], brecv.at[m], device_id=(y, t), device_id_type=MESH,
                ).start()
                return carry2

            lax.fori_loop(1, NE, send, 0)

        @pl.when(i < NC)
        def _():
            m = i

            @pl.when(m >= 2)
            def _():
                for c in grad_copies(m - 2):
                    c.wait()

            b = lax.rem(m, 2)
            xr = gath[m, 0].reshape(ROWS, CW)
            stg[b, 0] = tn(xr, ggi[...]).astype(BF16)
            stg[b, 1] = tn(xr, gui[...]).astype(BF16)
            stg[b, 2] = tn(hid[...], gath[m, 1].reshape(ROWS, CW)).astype(BF16)
            for c in grad_copies(m):
                c.start()

        @pl.when(i >= 3)
        def _():
            m = i - 3
            wait_plane(brecv.at[m])
            cols = pl.ds(mo(m * CW, CW), CW)
            blocks = back[m]
            lo_out[:, cols] = (nn(wout[0], blocks) + nn(wout[1], blocks)).astype(BF16)
            gt_out[:, cols] = nn(wout[2], blocks).astype(BF16)
            zacc[...] += nt(cot[:, cols], blocks)

        return carry

    lax.fori_loop(0, NC + 3, scatter_step, 0)

    z = zacc[...] * wout[3].astype(F32)
    owner = lax.broadcasted_iota(jnp.int32, (TOK, PR), 1) // BLK
    for k in range(TOP):
        gp_out[:, k : k + 1] = jnp.sum(jnp.where(owner == ids[:, k : k + 1], z, 0.0), axis=1, keepdims=True)

    for m in range(NC - 3, NC):
        sent(m)
        wait_plane(bsend.at[m])
    for m in range(NC - 2, NC):
        for c in grad_copies(m):
            c.wait()


def on_device(tokens, gate_probs, expert_ids, cotangent, w_gate, w_up, w_down):
    vm = pl.BlockSpec(memory_space=pltpu.VMEM)
    hbm = pl.BlockSpec(memory_space=pl.ANY)
    dma = pltpu.SemaphoreType.DMA
    flops = 9 * 2 * ROWS * D * FF
    lo, gt, gp, gg, gu, gd = pl.pallas_call(
        kernel,
        out_shape=(
            jax.ShapeDtypeStruct((TOK, D), BF16),
            jax.ShapeDtypeStruct((TOK, D), BF16),
            jax.ShapeDtypeStruct((TOK, TOP), F32),
            jax.ShapeDtypeStruct((D, FF), BF16),
            jax.ShapeDtypeStruct((D, FF), BF16),
            jax.ShapeDtypeStruct((FF, D), BF16),
        ),
        in_specs=[vm, vm, vm, vm, hbm, hbm, hbm],
        out_specs=(vm, vm, vm, hbm, hbm, hbm),
        scratch_shapes=[
            pltpu.VMEM((2 * NC * PR, CW), BF16),
            pltpu.VMEM((NC, 2, NY, SR, CW), BF16),
            pltpu.VMEM((NC, CW, FF), BF16),
            pltpu.VMEM((NC, CW, FF), BF16),
            pltpu.VMEM((NC, FF, CW), BF16),
            pltpu.VMEM((ROWS, FF), F32),
            pltpu.VMEM((ROWS, FF), F32),
            pltpu.VMEM((ROWS, FF), F32),
            pltpu.VMEM((ROWS, FF), BF16),
            pltpu.VMEM((ROWS, FF), BF16),
            pltpu.VMEM((ROWS, FF), BF16),
            pltpu.VMEM((NC, 2, SR, CW), BF16),
            pltpu.VMEM((NC, 2, 2, SR, CW), BF16),
            pltpu.VMEM((NC, PR, CW), BF16),
            pltpu.VMEM((2, 3, CW, FF), BF16),
            pltpu.VMEM((2, PR, TOK), BF16),
            pltpu.VMEM((PR, TOK), F32),
            pltpu.VMEM((4, TOK, PR), BF16),
            pltpu.VMEM((2 * SR, PR), BF16),
            pltpu.VMEM((TOK, PR), F32),
            dma((3, NC)), dma((NC,)), dma((NC,)),
            dma((2, 3, NC)), dma((2, 3, NC)), dma((2, 3, NC)), dma((2, 3, NC)),
            dma((NC,)), dma((NC,)), dma((3, NC)),
        ],
        compiler_params=pltpu.CompilerParams(
            collective_id=0, has_side_effects=True, vmem_limit_bytes=62 * 2**20
        ),
        cost_estimate=pl.CostEstimate(flops=flops, bytes_accessed=26 * 2**20, transcendentals=ROWS * FF),
    )(tokens, gate_probs, expert_ids, cotangent, w_gate[0], w_up[0], w_down[0])
    return lo, gt, gp, gg[None], gu[None], gd[None]


def solution(mesh):
    rows = P(("dp", "expert"), None)
    wide = P("expert", None, "dp")
    tall = P("expert", "dp", None)
    return jax.shard_map(
        on_device,
        mesh=mesh,
        in_specs=(rows, rows, rows, rows, wide, wide, tall),
        out_specs=(rows, rows, rows, wide, wide, tall),
        check_vma=False,
    )
```

```python
import jax
import jax.numpy as jnp
from jax import lax
from jax.experimental import pallas as pl
from jax.experimental.pallas import tpu as pltpu
from jax.sharding import PartitionSpec as P

MESH = pl.DeviceIdType.MESH
F32 = jnp.float32
BF16 = jnp.bfloat16

D = 3584
FF = 512
TOK = 128
TOP = 8
CAP = 6
NE = 32
NY = 4
NC = 7
CW = D // NC
NF = 3
NL = NC - NF
BLK = 16
FB = 48
HB = FB // 2
PR = NE * BLK
FR = NE * FB
SR = NE * CAP
ROWS = NY * SR
SL = 0
AL = SL + NL * PR
SF = AL + NL * PR
AF = SF + NF * FR
TB = AF + NF * FR
ST = TB + NF * 2 * NY * TOK
SA_ROWS = ST + 3 * CW
STAGE = AF + FR


def mo(v, m):
    return pl.multiple_of(v, m)


def nn(a, b):
    return lax.dot_general(a, b, (((1,), (0,)), ((), ())), preferred_element_type=F32)


def nt(a, b):
    return lax.dot_general(a, b, (((1,), (1,)), ((), ())), preferred_element_type=F32)


def tn(a, b):
    return lax.dot_general(a, b, (((0,), (0,)), ((), ())), preferred_element_type=F32)


def columns(c):
    return pl.ds(mo(c * CW, CW), CW)


def split3(v):
    a = v.astype(BF16)
    r = v - a.astype(F32)
    b = r.astype(BF16)
    return a, b, (r - b.astype(F32)).astype(BF16)


def kernel(
    tok, probs, ids, cot, wg_hbm, wu_hbm, wd_hbm,
    lo_hbm, gt_hbm, gp_out, gg_hbm, gu_hbm, gd_hbm,
    sa, gath, wg, wu, wd, accg, accu, acch, hid, ggi, gui,
    relay, vrec, relayf, vrecf, back, backf,
    gsel, psel, wout, pack, zacc, sel, pf, perm, zlane, idy, pry, zbuf,
    wsem, asend, arecv, ysend, yrecv, rsend, rrecv, bsend, brecv, gsem, osem, tsend, trecv, zsend, zrecv,
):
    y = lax.axis_index("dp")
    e = lax.axis_index("expert")
    right, left, across = lax.rem(y + 1, NY), lax.rem(y + 3, NY), lax.rem(y + 2, NY)
    sides = (right, left)
    ex, ez, ec = e // 8, lax.rem(e // 2, 4), lax.rem(e, 2)

    def peer(j):
        jx, jz, jc = lax.rem(j, 4), lax.rem(j // 4 + j, 4), j // 16
        return lax.rem(ex + jx, 4) * 8 + lax.rem(ez + jz, 4) * 2 + lax.rem(ec + jc, 2)

    barrier = pltpu.get_barrier_semaphore()
    for other in (right, left, across):
        pl.semaphore_signal(barrier, inc=1, device_id=(other, e), device_id_type=MESH)

    def greet(j, carry):
        pl.semaphore_signal(barrier, inc=1, device_id=(y, peer(j)), device_id_type=MESH)
        return carry

    lax.fori_loop(1, NE, greet, 0)

    def chunk_of(u):
        out = jnp.where(u < 2, u, jnp.where(u == 6, 2, u + 1))
        j = u - NC
        home = jnp.where(lax.rem(j, 2) == 0, NF + j // 2, (j - 1) // 2)
        return jnp.where(u < NC, out, home)

    def weight_copies(u):
        cols = columns(chunk_of(u))
        b = lax.rem(u, 2)
        return (
            pltpu.make_async_copy(wg_hbm.at[cols], wg.at[b], wsem.at[0, b]),
            pltpu.make_async_copy(wu_hbm.at[cols], wu.at[b], wsem.at[1, b]),
            pltpu.make_async_copy(wd_hbm.at[:, cols], wd.at[b], wsem.at[2, b]),
        )

    def load_weights(u):
        for c in weight_copies(u):
            c.start()

    load_weights(0)
    load_weights(1)

    def trow(n, kind, yy):
        return pl.ds(mo(TB + n * (2 * NY * TOK) + kind * (NY * TOK) + yy * TOK, TOK), TOK)

    def first_copy(n, kind, d):
        return pltpu.make_async_remote_copy(
            (tok, cot)[kind].at[:, columns(n)], sa.at[trow(n, kind, y)],
            ysend.at[d, kind, n], yrecv.at[d, kind, n], device_id=(sides[d], e), device_id_type=MESH,
        )

    def first_pass(n, d):
        ref = sa.at[trow(n, d, (left, right)[d])]
        return pltpu.make_async_remote_copy(
            ref, ref, ysend.at[d, 2, n], yrecv.at[d, 2, n], device_id=(sides[d], e), device_id_type=MESH,
        )

    def table_copies():
        return [
            pltpu.make_async_remote_copy(
                src, dst.at[y], tsend.at[k, t], trecv.at[k, t],
                device_id=((right, left, across)[t], e), device_id_type=MESH,
            )
            for t in range(3)
            for k, (src, dst) in enumerate(((ids, idy), (probs, pry)))
        ]

    pl.semaphore_wait(barrier, NE + 2)

    def start_first(n, carry):
        for kind in range(2):
            for d in range(2):
                first_copy(n, kind, d).start()
        return carry

    lax.fori_loop(0, NF, start_first, 0)
    for c in table_copies():
        c.start()

    esub = lax.broadcasted_iota(jnp.int32, (NE, TOK), 0)
    lane = lax.broadcasted_iota(jnp.int32, (TOK, TOK), 1)
    sub = lax.broadcasted_iota(jnp.int32, (TOK, TOK), 0)
    before = jnp.where(sub < lane, 1.0, 0.0).astype(BF16)

    def routing(ids_v, probs_v):
        named = jnp.zeros((NE, TOK), F32)
        weight = jnp.zeros((NE, TOK), F32)
        for k in range(TOP):
            hit = ids_v[k : k + 1, :] == esub
            named = named + jnp.where(hit, 1.0, 0.0)
            weight = weight + jnp.where(hit, probs_v[k : k + 1, :], 0.0)
        rank = nn(named.astype(BF16), before)
        return jnp.where(named > 0.5, rank, 255.0), weight

    def spread_rows(v, count):
        return jnp.broadcast_to(v[:, None, :], (NE, count, TOK)).reshape(NE * count, TOK)

    code0, weight0 = routing(ids[...], probs[...])
    code = spread_rows(code0, BLK)
    weight = spread_rows(weight0, BLK)
    place = lax.rem(lax.broadcasted_iota(jnp.int32, (PR, TOK), 0), BLK)
    slot = place.astype(F32)
    sel_x = jnp.where((place < CAP) & (code == slot), 1.0, 0.0)
    sel_c = jnp.where((place >= CAP) & (place < 2 * CAP) & (code == slot - CAP), 1.0, 0.0)
    gsel[0] = sel_x.astype(BF16)
    gsel[1] = sel_c.astype(BF16)
    psel[...] = jnp.broadcast_to(jnp.sum(sel_c * weight, axis=1, keepdims=True), (PR, TOK))

    def plane_send(src, dst, size, send_sem, recv_sem):
        def send(j, carry):
            t = peer(j)
            pltpu.make_async_remote_copy(
                src(t), dst, send_sem, recv_sem, device_id=(y, t), device_id_type=MESH
            ).start()
            return carry

        lax.fori_loop(1, NE, send, 0)

    def wait_plane(size, sem):
        blocks = sa.at[pl.ds(0, (NE - 1) * size)]
        pltpu.make_async_copy(blocks, blocks, sem).wait()

    def plane_out(l, carry):
        c = NF + l
        rows = nn(gsel[0], tok[:, columns(c)])
        crow = nn(gsel[1], cot[:, columns(c)])
        base = SL + l * PR
        sa[pl.ds(mo(base, PR), PR), :] = (rows + psel[:, 0:1] * crow).astype(BF16)
        mine = pl.ds(mo(AL + l * PR + e * BLK, BLK), BLK)
        sa[mine, :] = sa[pl.ds(mo(base + e * BLK, BLK), BLK), :]
        plane_send(
            lambda t: sa.at[pl.ds(mo(base + t * BLK, BLK), BLK)], sa.at[mine], BLK, asend.at[c], arecv.at[c]
        )
        return carry

    lax.fori_loop(0, NL, plane_out, 0)

    r_i = lax.broadcasted_iota(jnp.int32, (2 * SR, TOK), 0)
    q_i = lax.broadcasted_iota(jnp.int32, (2 * SR, TOK), 1)
    kind_i = jnp.where(r_i >= SR, 1, 0)
    r_i = r_i - kind_i * SR
    src_i = r_i // CAP
    target = src_i * BLK + kind_i * CAP + (r_i - src_i * CAP)
    for b in range(PR // TOK):
        pack[:, b * TOK : (b + 1) * TOK] = jnp.where(q_i + b * TOK == target, 1.0, 0.0).astype(BF16)
    zacc[...] = jnp.zeros((PR, TOK), F32)
    zlane[...] = jnp.zeros((ROWS, TOK), F32)

    def own_copy(c, kind, d):
        ref = gath.at[c, kind, y]
        return pltpu.make_async_remote_copy(
            ref, ref, ysend.at[d, kind, c], yrecv.at[d, kind, c], device_id=(sides[d], e), device_id_type=MESH,
        )

    def pass_copy(c, d):
        ref = gath.at[c, d, (left, right)[d]]
        return pltpu.make_async_remote_copy(
            ref, ref, ysend.at[d, 2, c], yrecv.at[d, 2, c], device_id=(sides[d], e), device_id_type=MESH,
        )

    def early(i, carry):
        @pl.when(i < NF)
        def _():
            for d in range(2):
                first_copy(i, d, d).wait_recv()
                first_pass(i, d).start()
            for d in range(2):
                first_copy(i, 1 - d, d).wait_recv()
            sa[trow(i, 0, y), :] = tok[:, columns(i)]
            sa[trow(i, 1, y), :] = cot[:, columns(i)]

        c = NF + i
        wait_plane(BLK, arecv.at[c])
        both = nn(pack[...], sa[pl.ds(mo(AL + i * PR, PR), PR), :]).astype(BF16)
        gath[c, 0, y] = both[:SR]
        gath[c, 1, y] = both[SR:]
        for kind in range(2):
            for d in range(2):
                own_copy(c, kind, d).start()
        return carry

    lax.fori_loop(0, NL, early, 0)

    for c in table_copies():
        c.wait_recv()
    idy[y] = ids[...]
    pry[y] = probs[...]
    fr_i = lax.rem(lax.broadcasted_iota(jnp.int32, (ROWS, TOK), 0), HB)
    p_rows = jnp.zeros((ROWS, 1), F32)
    for yy in range(NY):
        code_y, weight_y = routing(idy[yy], pry[yy])
        here = (fr_i >= yy * CAP) & (fr_i < (yy + 1) * CAP)
        one = jnp.where(here & (spread_rows(code_y, HB) == (fr_i - yy * CAP).astype(F32)), 1.0, 0.0)
        sel[:, yy * TOK : (yy + 1) * TOK] = one.astype(BF16)
        p_rows = p_rows + jnp.sum(one * spread_rows(weight_y, HB), axis=1, keepdims=True)
    pf[...] = jnp.broadcast_to(p_rows, (ROWS, TOK))

    def build_first(n, carry):
        for d in range(2):
            first_pass(n, d).wait_recv()
        mine = pl.ds(mo(AF + n * FR + e * FB, BLK), FB)
        base = SF + n * FR
        tx = sa[pl.ds(mo(TB + n * (2 * NY * TOK), TOK), NY * TOK), :]
        tc = sa[pl.ds(mo(TB + n * (2 * NY * TOK) + NY * TOK, TOK), NY * TOK), :]

        def quarter(q, carry2):
            rows = pl.ds(mo(q * SR, SR), SR)
            xr = nn(sel[rows, :], tx).reshape(8, HB, CW)
            cr = (pf[rows, 0:1] * nn(sel[rows, :], tc)).reshape(8, HB, CW)
            both = jnp.concatenate([xr, cr], axis=1).reshape(8 * FB, CW)
            sa[pl.ds(mo(base + q * (8 * FB), BLK), 8 * FB), :] = both.astype(BF16)
            return carry2

        lax.fori_loop(0, 4, quarter, 0)
        sa[mine, :] = sa[pl.ds(mo(base + e * FB, BLK), FB), :]
        plane_send(
            lambda t: sa.at[pl.ds(mo(base + t * FB, BLK), FB)], sa.at[mine], FB, asend.at[n], arecv.at[n]
        )
        return carry

    lax.fori_loop(0, NF, build_first, 0)

    r_i = lax.broadcasted_iota(jnp.int32, (ROWS, TOK), 0)
    q_i = lax.broadcasted_iota(jnp.int32, (ROWS, TOK), 1)
    y_i = r_i // SR
    r_i = r_i - y_i * SR
    src_i = r_i // CAP
    target = src_i * HB + y_i * CAP + (r_i - src_i * CAP)
    for b in range(ROWS // TOK):
        perm[:, b * TOK : (b + 1) * TOK] = jnp.where(q_i + b * TOK == target, 1.0, 0.0).astype(BF16)
    by_token = (sel_x * weight).T
    high = by_token.astype(BF16)
    wout[0] = high
    wout[1] = (by_token - high.astype(F32)).astype(BF16)
    wout[2] = sel_c.T.astype(BF16)
    accg[...] = jnp.zeros((ROWS, FF), F32)
    accu[...] = jnp.zeros((ROWS, FF), F32)
    acch[...] = jnp.zeros((ROWS, FF), F32)

    def halves(ref_rows, count):
        v = ref_rows.astype(F32).reshape(count, FB, CW)
        return v[:, :HB].reshape(count * HB, CW), v[:, HB:].reshape(count * HB, CW)

    def gather_step(u, carry):
        c = chunk_of(u)

        @pl.when(u < 2)
        def _():
            for h in range(2):
                l = NF + 2 * u + h
                for d in range(2):
                    own_copy(l, d, d).wait_recv()
                    pass_copy(l, d).start()
                for d in range(2):
                    own_copy(l, 1 - d, d).wait_recv()

        @pl.when((u < 2) | (u == 6))
        def _():
            wait_plane(FB, arecv.at[c])
            xs, cs = [], []
            for h in range(2):
                a, b = halves(sa[pl.ds(mo(AF + c * FR + h * (FR // 2), BLK), FR // 2), :], NE // 2)
                xs.append(a.astype(BF16))
                cs.append(b.astype(BF16))
            for kind, pieces in enumerate((xs, cs)):
                for h in range(2):
                    p = perm[h * 2 * SR : (h + 1) * 2 * SR, :]
                    rows = nn(p[:, : 2 * SR], pieces[0]) + nn(p[:, 2 * SR :], pieces[1])
                    gath[c, kind, 2 * h : 2 * h + 2] = rows.astype(BF16).reshape(2, SR, CW)

        @pl.when((u >= 2) & (u < 6))
        def _():
            for d in range(2):
                pass_copy(c, d).wait_recv()

        for w in weight_copies(u):
            w.wait()
        b = lax.rem(u, 2)

        def half(h, carry2):
            rows = pl.ds(mo(h * 2 * SR, 2 * SR), 2 * SR)
            xr = gath[c, 0, pl.ds(2 * h, 2)].reshape(2 * SR, CW)
            cr = gath[c, 1, pl.ds(2 * h, 2)].reshape(2 * SR, CW)
            accg[rows, :] += nn(xr, wg[b])
            accu[rows, :] += nn(xr, wu[b])
            acch[rows, :] += nt(cr, wd[b])
            return carry2

        lax.fori_loop(0, 2, half, 0)
        load_weights(u + 2)
        return carry

    lax.fori_loop(0, NC, gather_step, 0)

    def activate(i, carry):
        rows = pl.ds(mo(i * 32, 32), 32)
        g, u, h = accg[rows, :], accu[rows, :], acch[rows, :]
        s = jax.nn.sigmoid(g)
        act = g * s
        hid[rows, :] = (act * u).astype(BF16)
        gui[rows, :] = (h * act).astype(BF16)
        ggi[rows, :] = (h * u * s * (1.0 + g * (1.0 - s))).astype(BF16)
        return carry

    lax.fori_loop(0, ROWS // 32, activate, 0)

    def drain_plane(l, carry):
        wait_plane(BLK, asend.at[NF + l])
        return carry

    lax.fori_loop(0, NL, drain_plane, 0)

    def drain_early(n, carry):
        for d in range(2):
            for kind in range(2):
                first_copy(n, kind, d).wait_send()
            first_pass(n, d).wait_send()
        return carry

    lax.fori_loop(0, NF, drain_early, 0)

    def part_base(l):
        return jnp.where(l < 2, l * (2 * ROWS), AF + (l - 2) * (2 * ROWS))

    def part(l, kind, b):
        return pl.ds(mo(part_base(l) + kind * ROWS + b * SR, BLK), SR)

    def relay_copy(l, d):
        c = NF + l
        return pltpu.make_async_remote_copy(
            sa.at[part(l, d, across)], relay.at[l, d], rsend.at[d, 2, c], rrecv.at[d, 2, c],
            device_id=(sides[d], e), device_id_type=MESH,
        )

    def final_copy(l, kind, d):
        c = NF + l
        return pltpu.make_async_remote_copy(
            sa.at[part(l, kind, sides[d])], vrec.at[l, d, kind], rsend.at[d, kind, c], rrecv.at[d, kind, c],
            device_id=(sides[d], e), device_id_type=MESH,
        )

    def fpart(n, kind, b):
        return pl.ds(mo(SF + n * FR + b * (2 * TOK) + kind * TOK, TOK), TOK)

    def relay_first(n, d):
        return pltpu.make_async_remote_copy(
            sa.at[fpart(n, d, across)], relayf.at[n, d], rsend.at[d, 2, n], rrecv.at[d, 2, n],
            device_id=(sides[d], e), device_id_type=MESH,
        )

    def final_first(n, kind, d):
        return pltpu.make_async_remote_copy(
            sa.at[fpart(n, kind, sides[d])], vrecf.at[n, d, kind], rsend.at[d, kind, n], rrecv.at[d, kind, n],
            device_id=(sides[d], e), device_id_type=MESH,
        )

    def add_relay(l):
        for d in range(2):
            relay_copy(l, d).wait_recv()
            rows = part(l, d, sides[d])
            sa[rows, :] = (sa[rows, :].astype(F32) + relay[l, d].astype(F32)).astype(BF16)
            final_copy(l, d, d).start()

    def parts_step(j, carry):
        u = NC + j
        for w in weight_copies(u):
            w.wait()
        b = lax.rem(u, 2)
        plane_first = lax.rem(j, 2) == 0
        base = jnp.where(plane_first, part_base(j // 2), STAGE)

        def half(h, carry2):
            rows = pl.ds(mo(h * 2 * SR, 2 * SR), 2 * SR)
            at = base + h * 2 * SR
            sa[pl.ds(mo(at, BLK), 2 * SR), :] = nn(hid[rows, :], wd[b]).astype(BF16)
            dx = nt(ggi[rows, :], wg[b]) + nt(gui[rows, :], wu[b])
            sa[pl.ds(mo(at + ROWS, BLK), 2 * SR), :] = dx.astype(BF16)
            return carry2

        lax.fori_loop(0, 2, half, 0)

        @pl.when(u + 2 < 2 * NC)
        def _():
            load_weights(u + 2)

        @pl.when(plane_first)
        def _():
            l = j // 2
            for d in range(2):
                relay_copy(l, d).start()
            for d in range(2):
                final_copy(l, 1 - d, d).start()

        @pl.when(lax.rem(j, 2) == 1)
        def _():
            n = (j - 1) // 2
            wait_plane(FB, asend.at[n])
            first = SF + n * FR
            out_rows = sa[pl.ds(STAGE, ROWS), :]
            dx_rows = sa[pl.ds(STAGE + ROWS, ROWS), :]
            for h in range(2):
                p = perm[:, h * 2 * SR : (h + 1) * 2 * SR]
                o = tn(p, out_rows).reshape(NE // 2, HB, CW)
                d = tn(p, dx_rows).reshape(NE // 2, HB, CW)
                both = jnp.concatenate([o, d], axis=1).reshape(FR // 2, CW)
                sa[pl.ds(mo(first + h * (FR // 2), BLK), FR // 2), :] = both.astype(BF16)
            mine = pl.ds(mo(e * FB, BLK), FB)
            backf[n, mine, :] = sa[pl.ds(mo(first + e * FB, BLK), FB), :]
            plane_send(
                lambda t: sa.at[pl.ds(mo(first + t * FB, BLK), FB)], backf.at[n, mine], FB,
                bsend.at[n], brecv.at[n],
            )
            add_relay(n)

        return carry

    lax.fori_loop(0, NC, parts_step, 0)
    add_relay(NL - 1)

    def back_base(l):
        return jnp.where(l < 3, STAGE + 2 * ROWS + l * PR, 4 * ROWS)

    def to_plane(l):
        c = NF + l
        for d in range(2):
            for kind in range(2):
                final_copy(l, kind, d).wait_recv()
        total = []
        for kind in range(2):
            own = sa[part(l, kind, y), :].astype(F32)
            total.append((own + vrec[l, 0, kind].astype(F32) + vrec[l, 1, kind].astype(F32)).astype(BF16))
        base = back_base(l)
        spread = tn(pack[:SR, :], total[0]) + tn(pack[SR:, :], total[1])
        sa[pl.ds(mo(base, BLK), PR), :] = spread.astype(BF16)
        mine = pl.ds(mo(e * BLK, BLK), BLK)
        back[l, mine, :] = sa[pl.ds(mo(base + e * BLK, BLK), BLK), :]
        plane_send(
            lambda t: sa.at[pl.ds(mo(base + t * BLK, BLK), BLK)], back.at[l, mine], BLK, bsend.at[c], brecv.at[c]
        )

    def sum_tokens(n):
        wait_plane(FB, brecv.at[n])
        wait_plane(FB, bsend.at[n])
        tc = sa[pl.ds(mo(TB + n * (2 * NY * TOK) + NY * TOK, TOK), NY * TOK), :]
        lo = jnp.zeros((NY * TOK, CW), F32)
        gt = jnp.zeros((NY * TOK, CW), F32)
        for h in range(2):
            o, d = halves(backf[n, h * (FR // 2) : (h + 1) * (FR // 2), :], NE // 2)
            rows = slice(h * 2 * SR, (h + 1) * 2 * SR)
            s = sel[rows, :]
            prod = nn(s, tc) * o
            z = prod[:, :TOK]
            for q in range(1, CW // TOK):
                z = z + prod[:, q * TOK : (q + 1) * TOK]
            zlane[rows, :] += z
            lo = lo + tn(s, (pf[rows, 0:1] * o).astype(BF16))
            gt = gt + tn(s, d.astype(BF16))
        for yy in range(NY):
            sa[fpart(n, 0, yy), :] = lo[yy * TOK : (yy + 1) * TOK].astype(BF16)
            sa[fpart(n, 1, yy), :] = gt[yy * TOK : (yy + 1) * TOK].astype(BF16)
        for d in range(2):
            relay_first(n, d).start()
        for d in range(2):
            final_first(n, 1 - d, d).start()

    def staged(m, k):
        return pl.ds(mo(jnp.where(lax.rem(m, 2) == 0, ST + k * CW, TB + k * (2 * NY * TOK)), CW), CW)

    def grad_copies(m):
        cols = columns(m)
        return (
            pltpu.make_async_copy(sa.at[staged(m, 0)], gg_hbm.at[cols], gsem.at[0, m]),
            pltpu.make_async_copy(sa.at[staged(m, 1)], gu_hbm.at[cols], gsem.at[1, m]),
            pltpu.make_async_copy(sa.at[staged(m, 2)], gd_hbm.at[:, cols], gsem.at[2, m]),
        )

    def scatter_step(i, carry):
        @pl.when((lax.rem(i, 2) == 1) & (i < 6))
        def _():
            sum_tokens((i - 1) // 2)

        @pl.when((lax.rem(i, 2) == 0) & (i >= 2))
        def _():
            n = i // 2 - 1
            for d in range(2):
                relay_first(n, d).wait_recv()
                rows = fpart(n, d, sides[d])
                sa[rows, :] = (sa[rows, :].astype(F32) + relayf[n, d].astype(F32)).astype(BF16)
                final_first(n, d, d).start()

        @pl.when(i < NL)
        def _():
            to_plane(i)

        @pl.when(i >= 2)
        def _():
            for c in grad_copies(i - 2):
                c.wait()

        xr = gath[i, 0].reshape(ROWS, CW)
        sa[staged(i, 0), :] = tn(xr, ggi[...]).astype(BF16)
        sa[staged(i, 1), :] = tn(xr, gui[...]).astype(BF16)
        sa[staged(i, 2), :] = tn(hid[...], gath[i, 1].reshape(ROWS, CW)).astype(BF16)
        for c in grad_copies(i):
            c.start()
        return carry

    lax.fori_loop(0, NC, scatter_step, 0)

    def score_copies():
        return [
            pltpu.make_async_remote_copy(
                zbuf.at[3], zbuf.at[t], zsend.at[t], zrecv.at[t],
                device_id=((right, left, across)[t], e), device_id_type=MESH,
            )
            for t in range(3)
        ]

    ones = jnp.ones((8, TOK), BF16)
    z0, z1, z2 = split3(zlane[...])
    zbuf[3] = nt(ones, z0) + nt(ones, z1) + nt(ones, z2)
    for c in score_copies():
        c.start()

    def result_copy(blocks, c, kind):
        out = (lo_hbm, gt_hbm)[kind].at[:, columns(c)]
        return pltpu.make_async_copy(blocks.at[pl.ds(kind * TOK, TOK)], out, osem.at[kind, c])

    def last_first(n, carry):
        for d in range(2):
            for kind in range(2):
                final_first(n, kind, d).wait_recv()
        for kind in range(2):
            own = sa[fpart(n, kind, y), :].astype(F32)
            total = own + vrecf[n, 0, kind].astype(F32) + vrecf[n, 1, kind].astype(F32)
            backf[n, kind * TOK : (kind + 1) * TOK, :] = total.astype(BF16)
            result_copy(backf.at[n], n, kind).start()
        return carry

    lax.fori_loop(0, NF - 1, last_first, 0)

    def last_plane(l, carry):
        c = NF + l
        wait_plane(BLK, brecv.at[c])
        blocks = back[l]
        lo = nn(wout[0], blocks) + nn(wout[1], blocks)
        gt = nn(wout[2], blocks)
        zacc[...] += nt(blocks, cot[:, columns(c)])
        for kind, v in enumerate((lo, gt)):
            back[l, kind * TOK : (kind + 1) * TOK, :] = v.astype(BF16)
            result_copy(back.at[l], c, kind).start()
        return carry

    lax.fori_loop(0, NL, last_plane, 0)
    lax.fori_loop(NF - 1, NF, last_first, 0)

    for c in score_copies():
        c.wait_recv()
    zrow = (zbuf[3] + zbuf[0]) + (zbuf[1] + zbuf[2])
    zrow = jnp.broadcast_to(zrow[0:1], (NE, ROWS))
    group = lax.broadcasted_iota(jnp.int32, (NE, ROWS), 1) - HB * lax.broadcasted_iota(jnp.int32, (NE, ROWS), 0)
    z0, z1, z2 = split3(jnp.where((group >= 0) & (group < HB), zrow, 0.0))
    mine = sel[:, pl.ds(mo(y * TOK, TOK), TOK)]
    score = nn(z0, mine) + nn(z1, mine) + nn(z2, mine)
    score = score + jnp.sum((zacc[...] * gsel[0].astype(F32)).reshape(NE, BLK, TOK), axis=1)
    for k in range(TOP):
        gp_out[k : k + 1, :] = jnp.sum(jnp.where(ids[k : k + 1, :] == esub, score, 0.0), axis=0, keepdims=True)

    def drain(c, carry):
        for d in range(2):
            for kind in range(2):
                own_copy(c, kind, d).wait_send()
                final_copy(c - NF, kind, d).wait_send()
            pass_copy(c, d).wait_send()
            relay_copy(c - NF, d).wait_send()
        wait_plane(BLK, bsend.at[c])
        for kind in range(2):
            result_copy(back.at[c - NF], c, kind).wait()
        return carry

    lax.fori_loop(NF, NC, drain, 0)

    def drain_first(n, carry):
        for d in range(2):
            for kind in range(2):
                final_first(n, kind, d).wait_send()
            relay_first(n, d).wait_send()
        for kind in range(2):
            result_copy(backf.at[n], n, kind).wait()
        return carry

    lax.fori_loop(0, NF, drain_first, 0)
    for c in table_copies() + score_copies():
        c.wait_send()
    for m in range(NC - 2, NC):
        for c in grad_copies(m):
            c.wait()


def on_device(tokens, gate_probs, expert_ids, cotangent, w_gate, w_up, w_down):
    vm = pl.BlockSpec(memory_space=pltpu.VMEM)
    hbm = pl.BlockSpec(memory_space=pl.ANY)
    dma = pltpu.SemaphoreType.DMA
    flops = 9 * 2 * ROWS * D * FF
    lo, gt, gp, gg, gu, gd = pl.pallas_call(
        kernel,
        out_shape=(
            jax.ShapeDtypeStruct((TOK, D), BF16),
            jax.ShapeDtypeStruct((TOK, D), BF16),
            jax.ShapeDtypeStruct((TOP, TOK), F32),
            jax.ShapeDtypeStruct((D, FF), BF16),
            jax.ShapeDtypeStruct((D, FF), BF16),
            jax.ShapeDtypeStruct((FF, D), BF16),
        ),
        in_specs=[vm, vm, vm, vm, hbm, hbm, hbm],
        out_specs=(hbm, hbm, vm, hbm, hbm, hbm),
        scratch_shapes=[
            pltpu.VMEM((SA_ROWS, CW), BF16),
            pltpu.VMEM((NC, 2, NY, SR, CW), BF16),
            pltpu.VMEM((2, CW, FF), BF16),
            pltpu.VMEM((2, CW, FF), BF16),
            pltpu.VMEM((2, FF, CW), BF16),
            pltpu.VMEM((ROWS, FF), F32),
            pltpu.VMEM((ROWS, FF), F32),
            pltpu.VMEM((ROWS, FF), F32),
            pltpu.VMEM((ROWS, FF), BF16),
            pltpu.VMEM((ROWS, FF), BF16),
            pltpu.VMEM((ROWS, FF), BF16),
            pltpu.VMEM((NL, 2, SR, CW), BF16),
            pltpu.VMEM((NL, 2, 2, SR, CW), BF16),
            pltpu.VMEM((NF, 2, TOK, CW), BF16),
            pltpu.VMEM((NF, 2, 2, TOK, CW), BF16),
            pltpu.VMEM((NL, PR, CW), BF16),
            pltpu.VMEM((NF, FR, CW), BF16),
            pltpu.VMEM((2, PR, TOK), BF16),
            pltpu.VMEM((PR, TOK), F32),
            pltpu.VMEM((3, TOK, PR), BF16),
            pltpu.VMEM((2 * SR, PR), BF16),
            pltpu.VMEM((PR, TOK), F32),
            pltpu.VMEM((ROWS, NY * TOK), BF16),
            pltpu.VMEM((ROWS, TOK), F32),
            pltpu.VMEM((ROWS, ROWS), BF16),
            pltpu.VMEM((ROWS, TOK), F32),
            pltpu.VMEM((NY, TOP, TOK), jnp.int32),
            pltpu.VMEM((NY, TOP, TOK), F32),
            pltpu.VMEM((4, 8, ROWS), F32),
            dma((3, 2)), dma((NC,)), dma((NC,)),
            dma((2, 3, NC)), dma((2, 3, NC)), dma((2, 3, NC)), dma((2, 3, NC)),
            dma((NC,)), dma((NC,)), dma((3, NC)), dma((2, NC)),
            dma((2, 3)), dma((2, 3)), dma((3,)), dma((3,)),
        ],
        compiler_params=pltpu.CompilerParams(
            collective_id=0, has_side_effects=True, vmem_limit_bytes=int(63.5 * 2**20)
        ),
        cost_estimate=pl.CostEstimate(flops=flops, bytes_accessed=37 * 2**20, transcendentals=ROWS * FF),
    )(tokens, gate_probs.T, expert_ids.T, cotangent, w_gate[0], w_up[0], w_down[0])
    return lo, gt, gp.T, gg[None], gu[None], gd[None]


def solution(mesh):
    rows = P(("dp", "expert"), None)
    wide = P("expert", None, "dp")
    tall = P("expert", "dp", None)
    return jax.shard_map(
        on_device,
        mesh=mesh,
        in_specs=(rows, rows, rows, rows, wide, wide, tall),
        out_specs=(rows, rows, rows, wide, wide, tall),
        check_vma=False,
    )
```

```python
import jax
import jax.numpy as jnp
from jax import lax
from jax.experimental import pallas as pl
from jax.experimental.pallas import tpu as pltpu
from jax.sharding import PartitionSpec as P

MESH = pl.DeviceIdType.MESH
F32 = jnp.float32
BF16 = jnp.bfloat16

D = 3584
FF = 512
TOK = 128
TOP = 8
CAP = 6
NE = 32
NY = 4
NC = 7
CW = D // NC
NF = 3
NL = NC - NF
BLK = 16
FB = 48
HB = FB // 2
NX = NF + 1
FR = NE * FB
SR = NE * CAP
ROWS = NY * SR
TR = 2 * NY * TOK
AF = NX * FR
TB = 2 * NX * FR
ST = TB + NX * TR
SA_ROWS = ST + 3 * CW
LARGE, PIECES = 5, 4
PB = NF * FR
STAGE = PB + NL * FR


def mo(v, m):
    return pl.multiple_of(v, m)


def nn(a, b):
    return lax.dot_general(a, b, (((1,), (0,)), ((), ())), preferred_element_type=F32)


def nt(a, b):
    return lax.dot_general(a, b, (((1,), (1,)), ((), ())), preferred_element_type=F32)


def tn(a, b):
    return lax.dot_general(a, b, (((0,), (0,)), ((), ())), preferred_element_type=F32)


def columns(c):
    return pl.ds(mo(c * CW, CW), CW)


def split3(v):
    a = v.astype(BF16)
    r = v - a.astype(F32)
    b = r.astype(BF16)
    return a, b, (r - b.astype(F32)).astype(BF16)


def kernel(
    tok_hbm, probs, ids, cot_hbm, wg_hbm, wu_hbm, wd_hbm,
    lo_hbm, gt_hbm, gp_out, gg_hbm, gu_hbm, gd_hbm,
    sa, gath, wg, wu, wd, accg, accu, acch, hid, ggi, gui,
    relay, vrec, relayf, vrecf, backf,
    sel, pf, perm, idy, pry, zbuf, tok, cot,
    wsem, asend, arecv, ysend, yrecv, rsend, rrecv, bsend, brecv, gsem, osem, tsend, trecv, zsend, zrecv, isem,
):
    inputs = (
        pltpu.make_async_copy(tok_hbm, tok, isem.at[0]),
        pltpu.make_async_copy(cot_hbm, cot, isem.at[1]),
    )
    for c in inputs:
        c.start()
    y = lax.axis_index("dp")
    e = lax.axis_index("expert")
    right, left, across = lax.rem(y + 1, NY), lax.rem(y + 3, NY), lax.rem(y + 2, NY)
    sides = (right, left)
    ex, ez, ec = e // 8, lax.rem(e // 2, 4), lax.rem(e, 2)

    def peer(j):
        jx, jz, jc = lax.rem(j, 4), lax.rem(j // 4 + j, 4), j // 16
        return lax.rem(ex + jx, 4) * 8 + lax.rem(ez + jz, 4) * 2 + lax.rem(ec + jc, 2)

    barrier = pltpu.get_barrier_semaphore()
    for other in (right, left, across):
        pl.semaphore_signal(barrier, inc=1, device_id=(other, e), device_id_type=MESH)

    by_x = [lax.rem(ex + j, 4) * 8 for j in range(4)]
    by_z = [lax.rem(ez + j, 4) * 2 for j in range(4)]
    for j in range(1, NE):
        t = by_x[j % 4] + by_z[j // 4 % 4] + (ec if j < 16 else 1 - ec)
        pl.semaphore_signal(barrier, inc=1, device_id=(y, t), device_id_type=MESH)

    def chunk_of(u):
        out = jnp.where(u < 2, u, jnp.where(u == 6, 2, u + 1))
        j = u - NC
        home = jnp.where(lax.rem(j, 2) == 0, NF + j // 2, (j - 1) // 2)
        return jnp.where(u < NC, out, home)

    def weight_copies(u):
        cols = columns(chunk_of(u))
        b = lax.rem(u, 2)
        return (
            pltpu.make_async_copy(wg_hbm.at[cols], wg.at[b], wsem.at[0, b]),
            pltpu.make_async_copy(wu_hbm.at[cols], wu.at[b], wsem.at[1, b]),
            pltpu.make_async_copy(wd_hbm.at[:, cols], wd.at[b], wsem.at[2, b]),
        )

    def load_weights(u):
        for c in weight_copies(u):
            c.start()

    load_weights(0)
    load_weights(1)

    def trow(q, kind, g):
        return pl.ds(mo(TB + q * TR + kind * (NY * TOK) + g * TOK, TOK), TOK)

    def first_copy(n, kind, d):
        return pltpu.make_async_remote_copy(
            (tok, cot)[kind].at[:, columns(n)], sa.at[trow(n, kind, y)],
            ysend.at[d, kind, n], yrecv.at[d, kind, n], device_id=(sides[d], e), device_id_type=MESH,
        )

    def first_pass(n, d):
        ref = sa.at[trow(n, d, (left, right)[d])]
        return pltpu.make_async_remote_copy(
            ref, ref, ysend.at[d, 2, n], yrecv.at[d, 2, n], device_id=(sides[d], e), device_id_type=MESH,
        )

    def table_copies():
        return [
            pltpu.make_async_remote_copy(
                src, dst.at[y], tsend.at[k, t], trecv.at[k, t],
                device_id=((right, left, across)[t], e), device_id_type=MESH,
            )
            for t in range(3)
            for k, (src, dst) in enumerate(((ids, idy), (probs, pry)))
        ]

    def start_first(n, carry):
        for kind in range(2):
            for d in range(2):
                first_copy(n, kind, d).start()
        return carry

    for c in inputs:
        c.wait()
    pl.semaphore_wait(barrier, NE + 2)
    lax.fori_loop(0, NF, start_first, 0)
    for c in table_copies():
        c.start()

    esub = lax.broadcasted_iota(jnp.int32, (NE, TOK), 0)
    lane = lax.broadcasted_iota(jnp.int32, (TOK, TOK), 1)
    sub = lax.broadcasted_iota(jnp.int32, (TOK, TOK), 0)
    before = jnp.where(sub < lane, 1.0, 0.0).astype(BF16)

    def routing(ids_v, probs_v):
        named = jnp.zeros((NE, TOK), F32)
        weight = jnp.zeros((NE, TOK), F32)
        for k in range(TOP):
            hit = ids_v[k : k + 1, :] == esub
            named = named + jnp.where(hit, 1.0, 0.0)
            weight = weight + jnp.where(hit, probs_v[k : k + 1, :], 0.0)
        rank = nn(named.astype(BF16), before)
        return jnp.where(named > 0.5, rank, 255.0), weight

    def spread_rows(v, count):
        return jnp.broadcast_to(v[:, None, :], (NE, count, TOK)).reshape(NE * count, TOK)

    fr_i = lax.rem(lax.broadcasted_iota(jnp.int32, (ROWS, TOK), 0), HB)

    def place(k, tables):
        p_rows = jnp.zeros((ROWS, 1), F32)
        for g, (code_g, weight_g) in enumerate(tables):
            here = (fr_i >= g * CAP) & (fr_i < (g + 1) * CAP)
            one = jnp.where(here & (spread_rows(code_g, HB) == (fr_i - g * CAP).astype(F32)), 1.0, 0.0)
            sel[k, :, g * TOK : (g + 1) * TOK] = one.astype(BF16)
            p_rows = p_rows + jnp.sum(one * spread_rows(weight_g, HB), axis=1, keepdims=True)
        pf[k] = jnp.broadcast_to(p_rows, (ROWS, TOK))

    own_table = routing(ids[...], probs[...])

    def stack(c, carry):
        q, g = jnp.minimum(c, NF), jnp.where(c < NF, y, c - NF)
        sa[trow(q, 0, g), :] = tok[:, columns(c)]
        sa[trow(q, 1, g), :] = cot[:, columns(c)]
        return carry

    lax.fori_loop(NF, NC, stack, 0)
    place(1, [own_table] * NL)

    def plane_send(base, arrival, send_sem, recv_sem):
        def send(j, carry):
            t = peer(j)
            pltpu.make_async_remote_copy(
                sa.at[pl.ds(mo(base + t * FB, BLK), FB)], arrival, send_sem, recv_sem,
                device_id=(y, t), device_id_type=MESH,
            ).start()
            return carry

        lax.fori_loop(1, NE, send, 0)

    def wait_plane(sem):
        blocks = sa.at[pl.ds(0, (NE - 1) * FB)]
        pltpu.make_async_copy(blocks, blocks, sem).wait()

    def build(q, k):
        mine = pl.ds(mo(AF + q * FR + e * FB, BLK), FB)
        base = q * FR
        tx = sa[pl.ds(mo(TB + q * TR, TOK), NY * TOK), :]
        tc = sa[pl.ds(mo(TB + q * TR + NY * TOK, TOK), NY * TOK), :]

        def quarter(i, carry2):
            rows = pl.ds(mo(i * SR, SR), SR)
            xr = nn(sel[k, rows, :], tx).reshape(8, HB, CW)
            cr = (pf[k, rows, 0:1] * nn(sel[k, rows, :], tc)).reshape(8, HB, CW)
            both = jnp.concatenate([xr, cr], axis=1).reshape(8 * FB, CW)
            sa[pl.ds(mo(base + i * (8 * FB), BLK), 8 * FB), :] = both.astype(BF16)
            return carry2

        lax.fori_loop(0, 4, quarter, 0)
        sa[mine, :] = sa[pl.ds(mo(base + e * FB, BLK), FB), :]
        plane_send(base, sa.at[mine], asend.at[q], arecv.at[q])

    build(NF, 1)
    lax.fori_loop(0, NF, stack, 0)

    r_i = lax.broadcasted_iota(jnp.int32, (ROWS, TOK), 0)
    q_i = lax.broadcasted_iota(jnp.int32, (ROWS, TOK), 1)
    y_i = r_i // SR
    r_i = r_i - y_i * SR
    src_i = r_i // CAP
    target = src_i * HB + y_i * CAP + (r_i - src_i * CAP)
    for b in range(ROWS // TOK):
        perm[:, b * TOK : (b + 1) * TOK] = jnp.where(q_i + b * TOK == target, 1.0, 0.0).astype(BF16)
    accg[...] = jnp.zeros((ROWS, FF), F32)
    accu[...] = jnp.zeros((ROWS, FF), F32)
    acch[...] = jnp.zeros((ROWS, FF), F32)

    def own_copy(c, kind, d):
        ref = gath.at[c, kind, y]
        return pltpu.make_async_remote_copy(
            ref, ref, ysend.at[d, kind, c], yrecv.at[d, kind, c], device_id=(sides[d], e), device_id_type=MESH,
        )

    def pass_copy(c, d):
        ref = gath.at[c, d, (left, right)[d]]
        return pltpu.make_async_remote_copy(
            ref, ref, ysend.at[d, 2, c], yrecv.at[d, 2, c], device_id=(sides[d], e), device_id_type=MESH,
        )

    def early(i, carry):
        for d in range(2):
            first_copy(i, d, d).wait_recv()
            first_pass(i, d).start()
        for d in range(2):
            first_copy(i, 1 - d, d).wait_recv()
        return carry

    lax.fori_loop(0, NF, early, 0)

    for c in table_copies():
        c.wait_recv()
    idy[y] = ids[...]
    pry[y] = probs[...]
    place(0, [routing(idy[g], pry[g]) for g in range(NY)])

    def halves(ref_rows, count):
        v = ref_rows.astype(F32).reshape(count, FB, CW)
        return v[:, :HB].reshape(count * HB, CW), v[:, HB:].reshape(count * HB, CW)

    def arrived(q, store):
        wait_plane(arecv.at[q])
        xs, cs = [], []
        for h in range(2):
            a, b = halves(sa[pl.ds(mo(AF + q * FR + h * (FR // 2), BLK), FR // 2), :], NE // 2)
            xs.append(a.astype(BF16))
            cs.append(b.astype(BF16))
        for kind, pieces in enumerate((xs, cs)):
            for h in range(2):
                p = perm[h * 2 * SR : (h + 1) * 2 * SR, :]
                rows = nn(p[:, : 2 * SR], pieces[0]) + nn(p[:, 2 * SR :], pieces[1])
                store(kind, h, rows.astype(BF16).reshape(2, SR, CW))

    def keep_plane(kind, h, rows):
        for i in range(2):
            gath[NF + 2 * h + i, kind, y] = rows[i]

    arrived(NF, keep_plane)
    for c in range(NF, NC):
        for kind in range(2):
            for d in range(2):
                own_copy(c, kind, d).start()

    def build_first(n, carry):
        for d in range(2):
            first_pass(n, d).wait_recv()
        build(n, 0)
        return carry

    lax.fori_loop(0, NF, build_first, 0)

    def gather_step(u, carry):
        c = chunk_of(u)

        @pl.when(u < 2)
        def _():
            for h in range(2):
                l = NF + 2 * u + h
                for d in range(2):
                    own_copy(l, d, d).wait_recv()
                    pass_copy(l, d).start()
                for d in range(2):
                    own_copy(l, 1 - d, d).wait_recv()

        @pl.when(u < 2)
        def _():
            def keep_first(kind, h, rows):
                gath[c, kind, 2 * h : 2 * h + 2] = rows

            arrived(c, keep_first)

        @pl.when(u >= 2)
        def _():
            for d in range(2):
                pass_copy(c, d).wait_recv()

        for w in weight_copies(u):
            w.wait()
        b = lax.rem(u, 2)

        def half(h, carry2):
            rows = pl.ds(mo(h * 2 * SR, 2 * SR), 2 * SR)
            xr = gath[c, 0, pl.ds(2 * h, 2)].reshape(2 * SR, CW)
            cr = gath[c, 1, pl.ds(2 * h, 2)].reshape(2 * SR, CW)
            accg[rows, :] += nn(xr, wg[b])
            accu[rows, :] += nn(xr, wu[b])
            acch[rows, :] += nt(cr, wd[b])
            return carry2

        lax.fori_loop(0, 2, half, 0)
        @pl.when(u + 2 <= NC)
        def _():
            load_weights(u + 2)

        return carry

    lax.fori_loop(0, NC - 1, gather_step, 0)

    def keep_last_first(kind, h, rows):
        gath[NF - 1, kind, 2 * h : 2 * h + 2] = rows

    arrived(NF - 1, keep_last_first)
    for u in (NC - 1, NC):
        for w in weight_copies(u):
            w.wait()
    wait_plane(asend.at[NF])
    now, later = (NC - 1) % 2, NC % 2

    def part_base(l):
        return PB + l * FR

    def part(l, kind, b):
        return pl.ds(mo(part_base(l) + kind * ROWS + b * SR, BLK), SR)

    def relay_copy(l, d):
        c = NF + l
        return pltpu.make_async_remote_copy(
            sa.at[part(l, d, across)], relay.at[l, d], rsend.at[d, 2, c], rrecv.at[d, 2, c],
            device_id=(sides[d], e), device_id_type=MESH,
        )

    def final_copy(l, kind, d):
        c = NF + l
        return pltpu.make_async_remote_copy(
            sa.at[part(l, kind, sides[d])], vrec.at[l, d, kind], rsend.at[d, kind, c], rrecv.at[d, kind, c],
            device_id=(sides[d], e), device_id_type=MESH,
        )

    def fpart(n, kind, b):
        return pl.ds(mo(n * FR + b * (2 * TOK) + kind * TOK, TOK), TOK)

    def relay_first(n, d):
        return pltpu.make_async_remote_copy(
            sa.at[fpart(n, d, across)], relayf.at[n, d], rsend.at[d, 2, n], rrecv.at[d, 2, n],
            device_id=(sides[d], e), device_id_type=MESH,
        )

    def final_first(n, kind, d):
        return pltpu.make_async_remote_copy(
            sa.at[fpart(n, kind, sides[d])], vrecf.at[n, d, kind], rsend.at[d, kind, n], rrecv.at[d, kind, n],
            device_id=(sides[d], e), device_id_type=MESH,
        )

    def add_relay(l):
        for d in range(2):
            relay_copy(l, d).wait_recv()
            rows = part(l, d, sides[d])
            sa[rows, :] = (sa[rows, :].astype(F32) + relay[l, d].astype(F32)).astype(BF16)
            final_copy(l, d, d).start()

    def middle(step, carry):
        b = lax.rem(y + jnp.where(step == 0, 2, jnp.where(step == 2, 3, jnp.where(step == 3, 0, 1))), NY)
        rows = pl.ds(mo(b * SR, SR), SR)
        xr, cr = gath[NF - 1, 0, b], gath[NF - 1, 1, b]
        accg[rows, :] += nn(xr, wg[now])
        accu[rows, :] += nn(xr, wu[now])
        acch[rows, :] += nt(cr, wd[now])

        def activate(i, carry2):
            some = pl.ds(mo(b * SR + i * 32, 32), 32)
            g, u, h = accg[some, :], accu[some, :], acch[some, :]
            s = jax.nn.sigmoid(g)
            act = g * s
            hid[some, :] = (act * u).astype(BF16)
            gui[some, :] = (h * act).astype(BF16)
            ggi[some, :] = (h * u * s * (1.0 + g * (1.0 - s))).astype(BF16)
            return carry2

        lax.fori_loop(0, SR // 32, activate, 0)
        sa[part(0, 0, b), :] = nn(hid[rows, :], wd[later]).astype(BF16)
        sa[part(0, 1, b), :] = (nt(ggi[rows, :], wg[later]) + nt(gui[rows, :], wu[later])).astype(BF16)

        @pl.when(step == 0)
        def _():
            for d in range(2):
                relay_copy(0, d).start()

        for d in range(2):
            @pl.when(step == 1 + d)
            def _():
                final_copy(0, 1 - d, d).start()

        return carry

    lax.fori_loop(0, NY, middle, 0)
    load_weights(NC + 1)
    load_weights(NC + 2)
    accg[:, : 2 * TOK] = jnp.zeros((ROWS, 2 * TOK), F32)

    def drain_early(n, carry):
        for d in range(2):
            for kind in range(2):
                first_copy(n, kind, d).wait_send()
            first_pass(n, d).wait_send()
        return carry

    lax.fori_loop(0, NF, drain_early, 0)

    def send_back(q, base):
        out_rows = sa[pl.ds(STAGE, ROWS), :]
        dx_rows = sa[pl.ds(STAGE + ROWS, ROWS), :]
        for h in range(2):
            p = perm[:, h * 2 * SR : (h + 1) * 2 * SR]
            o = tn(p, out_rows).reshape(NE // 2, HB, CW)
            d = tn(p, dx_rows).reshape(NE // 2, HB, CW)
            both = jnp.concatenate([o, d], axis=1).reshape(FR // 2, CW)
            sa[pl.ds(mo(base + h * (FR // 2), BLK), FR // 2), :] = both.astype(BF16)
        mine = pl.ds(mo(e * FB, BLK), FB)
        backf[q, mine, :] = sa[pl.ds(mo(base + e * FB, BLK), FB), :]
        plane_send(base, backf.at[q, mine], bsend.at[q], brecv.at[q])

    def parts_step(j, carry):
        u = NC + j
        for w in weight_copies(u):
            w.wait()
        b = lax.rem(u, 2)
        plane_first = lax.rem(j, 2) == 0
        base = jnp.where(plane_first, part_base(j // 2), STAGE)

        def half(h, carry2):
            rows = pl.ds(mo(h * 2 * SR, 2 * SR), 2 * SR)
            at = base + h * 2 * SR
            sa[pl.ds(mo(at, BLK), 2 * SR), :] = nn(hid[rows, :], wd[b]).astype(BF16)
            dx = nt(ggi[rows, :], wg[b]) + nt(gui[rows, :], wu[b])
            sa[pl.ds(mo(at + ROWS, BLK), 2 * SR), :] = dx.astype(BF16)
            return carry2

        lax.fori_loop(0, 2, half, 0)

        @pl.when(u + 2 < 2 * NC)
        def _():
            load_weights(u + 2)

        @pl.when(plane_first)
        def _():
            l = j // 2
            for d in range(2):
                relay_copy(l, d).start()
            for d in range(2):
                final_copy(l, 1 - d, d).start()

        @pl.when(lax.rem(j, 2) == 1)
        def _():
            n = (j - 1) // 2
            wait_plane(asend.at[n])
            send_back(n, n * FR)
            add_relay(n)

        return carry

    lax.fori_loop(1, NC, parts_step, 0)
    add_relay(NL - 1)

    def to_plane(l):
        for d in range(2):
            for kind in range(2):
                final_copy(l, kind, d).wait_recv()
        for kind in range(2):
            own = sa[part(l, kind, y), :].astype(F32)
            total = own + vrec[l, 0, kind].astype(F32) + vrec[l, 1, kind].astype(F32)
            sa[pl.ds(mo(STAGE + kind * ROWS + l * SR, BLK), SR), :] = total.astype(BF16)

    def parts_sent(l):
        for d in range(2):
            for kind in range(2):
                final_copy(l, kind, d).wait_send()
            relay_copy(l, d).wait_send()

    def sum_tokens(q, k, store):
        wait_plane(brecv.at[q])
        tc = sa[pl.ds(mo(TB + q * TR + NY * TOK, TOK), NY * TOK), :]
        parts = (slice(0, ROWS // 2), slice(ROWS // 2, ROWS))

        def rows_of(h, kind):
            return halves(backf[q, h * (FR // 2) : (h + 1) * (FR // 2), :], NE // 2)[kind]

        for h, rows in enumerate(parts):
            prod = nn(sel[k, rows, :], tc) * rows_of(h, 0)
            z = prod[:, :TOK]
            for b in range(1, CW // TOK):
                z = z + prod[:, b * TOK : (b + 1) * TOK]
            accg[rows, k * TOK : (k + 1) * TOK] += z
        lo = [(pf[k, rows, 0:1] * rows_of(h, 0)).astype(BF16) for h, rows in enumerate(parts)]
        store(0, tn(sel[k, parts[0], :], lo[0]) + tn(sel[k, parts[1], :], lo[1]))
        gt = [rows_of(h, 1).astype(BF16) for h in range(2)]
        store(1, tn(sel[k, parts[0], :], gt[0]) + tn(sel[k, parts[1], :], gt[1]))

    def sum_first(n):
        wait_plane(bsend.at[n])

        def keep(kind, v):
            for g in range(NY):
                sa[fpart(n, kind, g), :] = v[g * TOK : (g + 1) * TOK].astype(BF16)

        sum_tokens(n, 0, keep)
        for d in range(2):
            relay_first(n, d).start()
        for d in range(2):
            final_first(n, 1 - d, d).start()

    def staged(m, k):
        return pl.ds(mo(jnp.where(lax.rem(m, 2) == 0, ST + k * CW, TB + k * TR), CW), CW)

    def grad_copies(m):
        cols = columns(m)
        return (
            pltpu.make_async_copy(sa.at[staged(m, 0)], gg_hbm.at[cols], gsem.at[0, m]),
            pltpu.make_async_copy(sa.at[staged(m, 1)], gu_hbm.at[cols], gsem.at[1, m]),
            pltpu.make_async_copy(sa.at[staged(m, 2)], gd_hbm.at[:, cols], gsem.at[2, m]),
        )

    def scatter_step(i, carry):
        @pl.when((lax.rem(i, 2) == 1) & (i < 6))
        def _():
            sum_first((i - 1) // 2)

        @pl.when((lax.rem(i, 2) == 0) & (i >= 2))
        def _():
            n = i // 2 - 1
            for d in range(2):
                relay_first(n, d).wait_recv()
                rows = fpart(n, d, sides[d])
                sa[rows, :] = (sa[rows, :].astype(F32) + relayf[n, d].astype(F32)).astype(BF16)
                final_first(n, d, d).start()

        @pl.when(i < NL)
        def _():
            to_plane(i)

        @pl.when(i == NL - 1)
        def _():
            parts_sent(0)
            send_back(NF, PB)

        @pl.when(i >= 2)
        def _():
            for c in grad_copies(i - 2):
                c.wait()

        xr = gath[i, 0].reshape(ROWS, CW)
        sa[staged(i, 0), :] = tn(xr, ggi[...]).astype(BF16)
        sa[staged(i, 1), :] = tn(xr, gui[...]).astype(BF16)
        sa[staged(i, 2), :] = tn(hid[...], gath[i, 1].reshape(ROWS, CW)).astype(BF16)
        for c in grad_copies(i):
            c.start()
        return carry

    lax.fori_loop(0, NC, scatter_step, 0)

    def score_copies():
        return [
            pltpu.make_async_remote_copy(
                zbuf.at[3], zbuf.at[t], zsend.at[t], zrecv.at[t],
                device_id=((right, left, across)[t], e), device_id_type=MESH,
            )
            for t in range(3)
        ]

    ones = jnp.ones((8, TOK), BF16)
    z0, z1, z2 = split3(accg[:, :TOK])
    zbuf[3] = nt(ones, z0) + nt(ones, z1) + nt(ones, z2)
    for c in score_copies():
        c.start()

    def result_copy(n, kind):
        out = (lo_hbm, gt_hbm)[kind].at[:, columns(n)]
        return pltpu.make_async_copy(backf.at[n, pl.ds(kind * TOK, TOK)], out, osem.at[kind, n])

    def last_copy(l, kind):
        rows = pl.ds(mo(STAGE + kind * (NY * TOK) + l * TOK, TOK), TOK)
        return pltpu.make_async_copy(sa.at[rows], (lo_hbm, gt_hbm)[kind].at[:, columns(NF + l)], osem.at[kind, NF + l])

    def last_first(n, carry):
        for d in range(2):
            for kind in range(2):
                final_first(n, kind, d).wait_recv()
        for kind in range(2):
            own = sa[fpart(n, kind, y), :].astype(F32)
            total = own + vrecf[n, 0, kind].astype(F32) + vrecf[n, 1, kind].astype(F32)
            backf[n, kind * TOK : (kind + 1) * TOK, :] = total.astype(BF16)
            result_copy(n, kind).start()
        return carry

    lax.fori_loop(0, NF, last_first, 0)

    def keep_last(kind, v):
        sa[pl.ds(STAGE + kind * NY * TOK, NY * TOK), :] = v.astype(BF16)
        for l in range(NL):
            last_copy(l, kind).start()

    sum_tokens(NF, 1, keep_last)

    for c in score_copies():
        c.wait_recv()
    zrow = (zbuf[3] + zbuf[0]) + (zbuf[1] + zbuf[2])
    group = lax.broadcasted_iota(jnp.int32, (NE, ROWS), 1) - HB * lax.broadcasted_iota(jnp.int32, (NE, ROWS), 0)
    group = (group >= 0) & (group < HB)
    z0, z1, z2 = split3(jnp.where(group, jnp.broadcast_to(zrow[0:1], (NE, ROWS)), 0.0))
    mine = sel[0, :, pl.ds(mo(y * TOK, TOK), TOK)]
    score = nn(z0, mine) + nn(z1, mine) + nn(z2, mine)
    z0, z1, z2 = split3(accg[:, TOK : 2 * TOK])
    zrow = nt(ones, z0) + nt(ones, z1) + nt(ones, z2)
    z0, z1, z2 = split3(jnp.where(group, jnp.broadcast_to(zrow[0:1], (NE, ROWS)), 0.0))
    for l in range(NL):
        mine = sel[1, :, l * TOK : (l + 1) * TOK]
        score = score + (nn(z0, mine) + nn(z1, mine) + nn(z2, mine))
    for k in range(TOP):
        gp_out[k : k + 1, :] = jnp.sum(jnp.where(ids[k : k + 1, :] == esub, score, 0.0), axis=0, keepdims=True)

    def drain(c, carry):
        l = c - NF
        for d in range(2):
            for kind in range(2):
                own_copy(c, kind, d).wait_send()
            pass_copy(c, d).wait_send()
        for kind in range(2):
            last_copy(l, kind).wait()

        @pl.when(l >= 1)
        def _():
            parts_sent(l)

        return carry

    lax.fori_loop(NF, NC, drain, 0)
    wait_plane(bsend.at[NF])

    def drain_first(n, carry):
        for d in range(2):
            for kind in range(2):
                final_first(n, kind, d).wait_send()
            relay_first(n, d).wait_send()
        for kind in range(2):
            result_copy(n, kind).wait()
        return carry

    lax.fori_loop(0, NF, drain_first, 0)
    for c in table_copies() + score_copies():
        c.wait_send()
    for m in range(NC - 2, NC):
        for c in grad_copies(m):
            c.wait()


def keep_kernel(*refs):
    small, small_out = refs[0], refs[LARGE + 1]
    small_out[...] = small[...]
    refs = refs[1 : LARGE + 1] + refs[LARGE + 2 :]
    count = LARGE
    rsem, wsem = refs[-2:]
    reads, writes = [], []
    for k in range(PIECES):
        for i in range(count):
            src, dst, held = refs[i], refs[count + i], refs[2 * count + i]
            step = src.shape[0] // PIECES
            rows = pl.ds(k * step, step)
            reads.append(pltpu.make_async_copy(src.at[rows], held.at[rows], rsem.at[i, k]))
            writes.append(pltpu.make_async_copy(held.at[rows], dst.at[rows], wsem.at[i, k]))
    for c in reads:
        c.start()
    for r, w in zip(reads, writes):
        r.wait()
        w.start()
    for w in writes:
        w.wait()


def keep(small, *arrays):
    vm = pl.BlockSpec(memory_space=pltpu.VMEM)
    hbm = pl.BlockSpec(memory_space=pl.ANY)
    sems = pltpu.SemaphoreType.DMA((LARGE, PIECES))
    return pl.pallas_call(
        keep_kernel,
        out_shape=tuple(jax.ShapeDtypeStruct(a.shape, a.dtype) for a in (small, *arrays)),
        in_specs=[vm] + [hbm] * LARGE,
        out_specs=(vm,) + (hbm,) * LARGE,
        scratch_shapes=[pltpu.VMEM(a.shape, a.dtype) for a in arrays] + [sems, sems],
        compiler_params=pltpu.CompilerParams(vmem_limit_bytes=63 * 2**20),
    )(small, *arrays)


def on_device(tokens, gate_probs, expert_ids, cotangent, w_gate, w_up, w_down):
    vm = pl.BlockSpec(memory_space=pltpu.VMEM)
    hbm = pl.BlockSpec(memory_space=pl.ANY)
    dma = pltpu.SemaphoreType.DMA
    flops = 9 * 2 * ROWS * D * FF
    lo, gt, gp, gg, gu, gd = pl.pallas_call(
        kernel,
        out_shape=(
            jax.ShapeDtypeStruct((TOK, D), BF16),
            jax.ShapeDtypeStruct((TOK, D), BF16),
            jax.ShapeDtypeStruct((TOP, TOK), F32),
            jax.ShapeDtypeStruct((D, FF), BF16),
            jax.ShapeDtypeStruct((D, FF), BF16),
            jax.ShapeDtypeStruct((FF, D), BF16),
        ),
        in_specs=[hbm, vm, vm, hbm, hbm, hbm, hbm],
        out_specs=(hbm, hbm, vm, hbm, hbm, hbm),
        scratch_shapes=[
            pltpu.VMEM((SA_ROWS, CW), BF16),
            pltpu.VMEM((NC, 2, NY, SR, CW), BF16),
            pltpu.VMEM((2, CW, FF), BF16),
            pltpu.VMEM((2, CW, FF), BF16),
            pltpu.VMEM((2, FF, CW), BF16),
            pltpu.VMEM((ROWS, FF), F32),
            pltpu.VMEM((ROWS, FF), F32),
            pltpu.VMEM((ROWS, FF), F32),
            pltpu.VMEM((ROWS, FF), BF16),
            pltpu.VMEM((ROWS, FF), BF16),
            pltpu.VMEM((ROWS, FF), BF16),
            pltpu.VMEM((NL, 2, SR, CW), BF16),
            pltpu.VMEM((NL, 2, 2, SR, CW), BF16),
            pltpu.VMEM((NF, 2, TOK, CW), BF16),
            pltpu.VMEM((NF, 2, 2, TOK, CW), BF16),
            pltpu.VMEM((NX, FR, CW), BF16),
            pltpu.VMEM((2, ROWS, NY * TOK), BF16),
            pltpu.VMEM((2, ROWS, TOK), F32),
            pltpu.VMEM((ROWS, ROWS), BF16),
            pltpu.VMEM((NY, TOP, TOK), jnp.int32),
            pltpu.VMEM((NY, TOP, TOK), F32),
            pltpu.VMEM((4, 8, ROWS), F32),
            pltpu.VMEM((TOK, D), BF16),
            pltpu.VMEM((TOK, D), BF16),
            dma((3, 2)), dma((NX,)), dma((NX,)),
            dma((2, 3, NC)), dma((2, 3, NC)), dma((2, 3, NC)), dma((2, 3, NC)),
            dma((NX,)), dma((NX,)), dma((3, NC)), dma((2, NC)),
            dma((2, 3)), dma((2, 3)), dma((3,)), dma((3,)), dma((2,)),
        ],
        compiler_params=pltpu.CompilerParams(
            collective_id=0, has_side_effects=True, vmem_limit_bytes=int(63.5 * 2**20)
        ),
        cost_estimate=pl.CostEstimate(flops=flops, bytes_accessed=37 * 2**20, transcendentals=ROWS * FF),
    )(tokens, gate_probs.T, expert_ids.T, cotangent, w_gate[0], w_up[0], w_down[0])
    gp, lo, gt, gg, gu, gd = keep(gp, lo, gt, gg, gu, gd)
    return lo, gt, gp.T, gg[None], gu[None], gd[None]


def solution(mesh):
    rows = P(("dp", "expert"), None)
    wide = P("expert", None, "dp")
    tall = P("expert", "dp", None)
    return jax.shard_map(
        on_device,
        mesh=mesh,
        in_specs=(rows, rows, rows, rows, wide, wide, tall),
        out_specs=(rows, rows, rows, wide, wide, tall),
        check_vma=False,
    )
```

```python
import jax
import jax.numpy as jnp
from jax import lax
from jax.experimental import pallas as pl
from jax.experimental.pallas import tpu as pltpu
from jax.sharding import PartitionSpec as P

MESH = pl.DeviceIdType.MESH
F32 = jnp.float32
BF16 = jnp.bfloat16

D = 3584
FF = 512
TOK = 128
TOP = 8
CAP = 6
NE = 32
NY = 4
NC = 7
CW = D // NC
NF = 3
NL = NC - NF
BLK = 16
FB = 48
HB = FB // 2
NX = NF + 1
FR = NE * FB
SR = NE * CAP
ROWS = NY * SR
TR = 2 * NY * TOK
AF = NX * FR
TB = 2 * NX * FR
SA_ROWS = TB + NX * TR
PB = NF * FR
STAGE = PB + NL * FR


def mo(v, m):
    return pl.multiple_of(v, m)


def nn(a, b):
    return lax.dot_general(a, b, (((1,), (0,)), ((), ())), preferred_element_type=F32)


def nt(a, b):
    return lax.dot_general(a, b, (((1,), (1,)), ((), ())), preferred_element_type=F32)


def tn(a, b):
    return lax.dot_general(a, b, (((0,), (0,)), ((), ())), preferred_element_type=F32)


def columns(c):
    return pl.ds(mo(c * CW, CW), CW)


def split3(v):
    a = v.astype(BF16)
    r = v - a.astype(F32)
    b = r.astype(BF16)
    return a, b, (r - b.astype(F32)).astype(BF16)


def kernel(
    tok_hbm, probs_hbm, ids_hbm, cot_hbm, wg_hbm, wu_hbm, wd_hbm,
    res, gp_out, gath,
    sa, wg, wu, wd, accg, accu, acch, hid, ggi, gui,
    relay, vrec, relayf, vrecf, backf,
    sel, pf, perm, idy, pry, zbuf, probs, ids,
    wsem, asend, arecv, ysend, yrecv, rsend, rrecv, bsend, brecv, tsend, trecv, zsend, zrecv, isem, tabsem,
):
    y = lax.axis_index("dp")
    e = lax.axis_index("expert")

    def trow(q, kind, g):
        return pl.ds(mo(TB + q * TR + kind * (NY * TOK) + g * TOK, TOK), TOK)

    def input_copies(c):
        q, g = jnp.minimum(c, NF), jnp.where(c < NF, y, c - NF)
        return (
            pltpu.make_async_copy(tok_hbm.at[:, columns(c)], sa.at[trow(q, 0, g)], isem.at[0, c]),
            pltpu.make_async_copy(cot_hbm.at[:, columns(c)], sa.at[trow(q, 1, g)], isem.at[1, c]),
        )

    def start_inputs(c, carry):
        for v in input_copies(c):
            v.start()
        return carry

    def wait_inputs(c, carry):
        for v in input_copies(c):
            v.wait()
        return carry

    lax.fori_loop(0, NC, start_inputs, 0)
    tables = (
        pltpu.make_async_copy(probs_hbm, probs, tabsem.at[0]),
        pltpu.make_async_copy(ids_hbm, ids, tabsem.at[1]),
    )
    for v in tables:
        v.start()
    right, left, across = lax.rem(y + 1, NY), lax.rem(y + 3, NY), lax.rem(y + 2, NY)
    sides = (right, left)
    ex, ez, ec = e // 8, lax.rem(e // 2, 4), lax.rem(e, 2)

    def peer(j):
        jx, jz, jc = lax.rem(j, 4), lax.rem(j // 4 + j, 4), j // 16
        return lax.rem(ex + jx, 4) * 8 + lax.rem(ez + jz, 4) * 2 + lax.rem(ec + jc, 2)

    barrier = pltpu.get_barrier_semaphore()
    for other in (right, left, across):
        pl.semaphore_signal(barrier, inc=1, device_id=(other, e), device_id_type=MESH)

    by_x = [lax.rem(ex + j, 4) * 8 for j in range(4)]
    by_z = [lax.rem(ez + j, 4) * 2 for j in range(4)]
    for j in range(1, NE):
        t = by_x[j % 4] + by_z[j // 4 % 4] + (ec if j < 16 else 1 - ec)
        pl.semaphore_signal(barrier, inc=1, device_id=(y, t), device_id_type=MESH)

    def chunk_of(u):
        out = jnp.where(u < 2, u, jnp.where(u == 6, 2, u + 1))
        j = u - NC
        home = jnp.where(lax.rem(j, 2) == 0, NF + j // 2, (j - 1) // 2)
        return jnp.where(u < NC, out, home)

    def weight_copies(u):
        cols = columns(chunk_of(u))
        b = lax.rem(u, 2)
        return (
            pltpu.make_async_copy(wg_hbm.at[cols], wg.at[b], wsem.at[0, b]),
            pltpu.make_async_copy(wu_hbm.at[cols], wu.at[b], wsem.at[1, b]),
            pltpu.make_async_copy(wd_hbm.at[:, cols], wd.at[b], wsem.at[2, b]),
        )

    def load_weights(u):
        for c in weight_copies(u):
            c.start()

    load_weights(0)
    load_weights(1)

    def first_copy(n, kind, d):
        return pltpu.make_async_remote_copy(
            sa.at[trow(n, kind, y)], sa.at[trow(n, kind, y)],
            ysend.at[d, kind, n], yrecv.at[d, kind, n], device_id=(sides[d], e), device_id_type=MESH,
        )

    def first_pass(n, d):
        ref = sa.at[trow(n, d, (left, right)[d])]
        return pltpu.make_async_remote_copy(
            ref, ref, ysend.at[d, 2, n], yrecv.at[d, 2, n], device_id=(sides[d], e), device_id_type=MESH,
        )

    def table_copies():
        return [
            pltpu.make_async_remote_copy(
                src, dst.at[y], tsend.at[k, t], trecv.at[k, t],
                device_id=((right, left, across)[t], e), device_id_type=MESH,
            )
            for t in range(3)
            for k, (src, dst) in enumerate(((ids, idy), (probs, pry)))
        ]

    def start_first(n, carry):
        for kind in range(2):
            for d in range(2):
                first_copy(n, kind, d).start()
        return carry

    lax.fori_loop(0, NC, wait_inputs, 0)
    for v in tables:
        v.wait()
    pl.semaphore_wait(barrier, NE + 2)
    lax.fori_loop(0, NF, start_first, 0)
    for c in table_copies():
        c.start()

    esub = lax.broadcasted_iota(jnp.int32, (NE, TOK), 0)
    lane = lax.broadcasted_iota(jnp.int32, (TOK, TOK), 1)
    sub = lax.broadcasted_iota(jnp.int32, (TOK, TOK), 0)
    before = jnp.where(sub < lane, 1.0, 0.0).astype(BF16)

    def routing(ids_v, probs_v):
        named = jnp.zeros((NE, TOK), F32)
        weight = jnp.zeros((NE, TOK), F32)
        for k in range(TOP):
            hit = ids_v[k : k + 1, :] == esub
            named = named + jnp.where(hit, 1.0, 0.0)
            weight = weight + jnp.where(hit, probs_v[k : k + 1, :], 0.0)
        rank = nn(named.astype(BF16), before)
        return jnp.where(named > 0.5, rank, 255.0), weight

    def spread_rows(v, count):
        return jnp.broadcast_to(v[:, None, :], (NE, count, TOK)).reshape(NE * count, TOK)

    fr_i = lax.rem(lax.broadcasted_iota(jnp.int32, (ROWS, TOK), 0), HB)

    def place(k, tables):
        p_rows = jnp.zeros((ROWS, 1), F32)
        for g, (code_g, weight_g) in enumerate(tables):
            here = (fr_i >= g * CAP) & (fr_i < (g + 1) * CAP)
            one = jnp.where(here & (spread_rows(code_g, HB) == (fr_i - g * CAP).astype(F32)), 1.0, 0.0)
            sel[k, :, g * TOK : (g + 1) * TOK] = one.astype(BF16)
            p_rows = p_rows + jnp.sum(one * spread_rows(weight_g, HB), axis=1, keepdims=True)
        pf[k] = jnp.broadcast_to(p_rows, (ROWS, TOK))

    own_table = routing(ids[...], probs[...])

    place(1, [own_table] * NL)

    def plane_send(base, arrival, send_sem, recv_sem):
        def send(j, carry):
            t = peer(j)
            pltpu.make_async_remote_copy(
                sa.at[pl.ds(mo(base + t * FB, BLK), FB)], arrival, send_sem, recv_sem,
                device_id=(y, t), device_id_type=MESH,
            ).start()
            return carry

        lax.fori_loop(1, NE, send, 0)

    def wait_plane(sem):
        blocks = sa.at[pl.ds(0, (NE - 1) * FB)]
        pltpu.make_async_copy(blocks, blocks, sem).wait()

    def build(q, k):
        mine = pl.ds(mo(AF + q * FR + e * FB, BLK), FB)
        base = q * FR
        tx = sa[pl.ds(mo(TB + q * TR, TOK), NY * TOK), :]
        tc = sa[pl.ds(mo(TB + q * TR + NY * TOK, TOK), NY * TOK), :]

        def quarter(i, carry2):
            rows = pl.ds(mo(i * SR, SR), SR)
            xr = nn(sel[k, rows, :], tx).reshape(8, HB, CW)
            cr = (pf[k, rows, 0:1] * nn(sel[k, rows, :], tc)).reshape(8, HB, CW)
            both = jnp.concatenate([xr, cr], axis=1).reshape(8 * FB, CW)
            sa[pl.ds(mo(base + i * (8 * FB), BLK), 8 * FB), :] = both.astype(BF16)
            return carry2

        lax.fori_loop(0, 4, quarter, 0)
        sa[mine, :] = sa[pl.ds(mo(base + e * FB, BLK), FB), :]
        plane_send(base, sa.at[mine], asend.at[q], arecv.at[q])

    build(NF, 1)

    r_i = lax.broadcasted_iota(jnp.int32, (ROWS, TOK), 0)
    q_i = lax.broadcasted_iota(jnp.int32, (ROWS, TOK), 1)
    y_i = r_i // SR
    r_i = r_i - y_i * SR
    src_i = r_i // CAP
    target = src_i * HB + y_i * CAP + (r_i - src_i * CAP)
    for b in range(ROWS // TOK):
        perm[:, b * TOK : (b + 1) * TOK] = jnp.where(q_i + b * TOK == target, 1.0, 0.0).astype(BF16)
    accg[...] = jnp.zeros((ROWS, FF), F32)
    accu[...] = jnp.zeros((ROWS, FF), F32)
    acch[...] = jnp.zeros((ROWS, FF), F32)

    def grow(c, kind, b):
        return pl.ds(mo(c * (2 * ROWS) + kind * ROWS + b * SR, BLK), SR)

    def gpair(c, kind, h):
        return pl.ds(mo(c * (2 * ROWS) + kind * ROWS + h * 2 * SR, BLK), 2 * SR)

    def own_copy(c, kind, d):
        ref = gath.at[grow(c, kind, y)]
        return pltpu.make_async_remote_copy(
            ref, ref, ysend.at[d, kind, c], yrecv.at[d, kind, c], device_id=(sides[d], e), device_id_type=MESH,
        )

    def pass_copy(c, d):
        ref = gath.at[grow(c, d, (left, right)[d])]
        return pltpu.make_async_remote_copy(
            ref, ref, ysend.at[d, 2, c], yrecv.at[d, 2, c], device_id=(sides[d], e), device_id_type=MESH,
        )

    def early(i, carry):
        for d in range(2):
            first_copy(i, d, d).wait_recv()
            first_pass(i, d).start()
        for d in range(2):
            first_copy(i, 1 - d, d).wait_recv()
        return carry

    lax.fori_loop(0, NF, early, 0)

    for c in table_copies():
        c.wait_recv()
    idy[y] = ids[...]
    pry[y] = probs[...]
    place(0, [routing(idy[g], pry[g]) for g in range(NY)])

    def halves(ref_rows, count):
        v = ref_rows.astype(F32).reshape(count, FB, CW)
        return v[:, :HB].reshape(count * HB, CW), v[:, HB:].reshape(count * HB, CW)

    def arrived(q, store):
        wait_plane(arecv.at[q])
        xs, cs = [], []
        for h in range(2):
            a, b = halves(sa[pl.ds(mo(AF + q * FR + h * (FR // 2), BLK), FR // 2), :], NE // 2)
            xs.append(a.astype(BF16))
            cs.append(b.astype(BF16))
        for kind, pieces in enumerate((xs, cs)):
            for h in range(2):
                p = perm[h * 2 * SR : (h + 1) * 2 * SR, :]
                rows = nn(p[:, : 2 * SR], pieces[0]) + nn(p[:, 2 * SR :], pieces[1])
                store(kind, h, rows.astype(BF16))

    def keep_plane(kind, h, rows):
        for i in range(2):
            gath[grow(NF + 2 * h + i, kind, y), :] = rows[i * SR : (i + 1) * SR]

    arrived(NF, keep_plane)
    for c in range(NF, NC):
        for kind in range(2):
            for d in range(2):
                own_copy(c, kind, d).start()

    def build_first(n, carry):
        for d in range(2):
            first_pass(n, d).wait_recv()
        build(n, 0)
        return carry

    lax.fori_loop(0, NF, build_first, 0)

    def gather_step(u, carry):
        c = chunk_of(u)

        @pl.when(u < 2)
        def _():
            for h in range(2):
                l = NF + 2 * u + h
                for d in range(2):
                    own_copy(l, d, d).wait_recv()
                    pass_copy(l, d).start()
                for d in range(2):
                    own_copy(l, 1 - d, d).wait_recv()

        @pl.when(u < 2)
        def _():
            def keep_first(kind, h, rows):
                gath[gpair(c, kind, h), :] = rows

            arrived(c, keep_first)

        @pl.when(u >= 2)
        def _():
            for d in range(2):
                pass_copy(c, d).wait_recv()

        for w in weight_copies(u):
            w.wait()
        b = lax.rem(u, 2)

        def half(h, carry2):
            rows = pl.ds(mo(h * 2 * SR, 2 * SR), 2 * SR)
            xr = gath[gpair(c, 0, h), :]
            cr = gath[gpair(c, 1, h), :]
            accg[rows, :] += nn(xr, wg[b])
            accu[rows, :] += nn(xr, wu[b])
            acch[rows, :] += nt(cr, wd[b])
            return carry2

        lax.fori_loop(0, 2, half, 0)
        @pl.when(u + 2 <= NC)
        def _():
            load_weights(u + 2)

        return carry

    lax.fori_loop(0, NC - 1, gather_step, 0)

    def keep_last_first(kind, h, rows):
        gath[gpair(NF - 1, kind, h), :] = rows

    arrived(NF - 1, keep_last_first)
    for u in (NC - 1, NC):
        for w in weight_copies(u):
            w.wait()
    wait_plane(asend.at[NF])
    now, later = (NC - 1) % 2, NC % 2

    def part_base(l):
        return PB + l * FR

    def part(l, kind, b):
        return pl.ds(mo(part_base(l) + kind * ROWS + b * SR, BLK), SR)

    def relay_copy(l, d):
        c = NF + l
        return pltpu.make_async_remote_copy(
            sa.at[part(l, d, across)], relay.at[l, d], rsend.at[d, 2, c], rrecv.at[d, 2, c],
            device_id=(sides[d], e), device_id_type=MESH,
        )

    def final_copy(l, kind, d):
        c = NF + l
        return pltpu.make_async_remote_copy(
            sa.at[part(l, kind, sides[d])], vrec.at[l, d, kind], rsend.at[d, kind, c], rrecv.at[d, kind, c],
            device_id=(sides[d], e), device_id_type=MESH,
        )

    def fpart(n, kind, b):
        return pl.ds(mo(n * FR + b * (2 * TOK) + kind * TOK, TOK), TOK)

    def relay_first(n, d):
        return pltpu.make_async_remote_copy(
            sa.at[fpart(n, d, across)], relayf.at[n, d], rsend.at[d, 2, n], rrecv.at[d, 2, n],
            device_id=(sides[d], e), device_id_type=MESH,
        )

    def final_first(n, kind, d):
        return pltpu.make_async_remote_copy(
            sa.at[fpart(n, kind, sides[d])], vrecf.at[n, d, kind], rsend.at[d, kind, n], rrecv.at[d, kind, n],
            device_id=(sides[d], e), device_id_type=MESH,
        )

    def add_relay(l):
        for d in range(2):
            relay_copy(l, d).wait_recv()
            rows = part(l, d, sides[d])
            sa[rows, :] = (sa[rows, :].astype(F32) + relay[l, d].astype(F32)).astype(BF16)
            final_copy(l, d, d).start()

    def middle(step, carry):
        b = lax.rem(y + jnp.where(step == 0, 2, jnp.where(step == 2, 3, jnp.where(step == 3, 0, 1))), NY)
        rows = pl.ds(mo(b * SR, SR), SR)
        xr, cr = gath[grow(NF - 1, 0, b), :], gath[grow(NF - 1, 1, b), :]
        accg[rows, :] += nn(xr, wg[now])
        accu[rows, :] += nn(xr, wu[now])
        acch[rows, :] += nt(cr, wd[now])

        def activate(i, carry2):
            some = pl.ds(mo(b * SR + i * 32, 32), 32)
            g, u, h = accg[some, :], accu[some, :], acch[some, :]
            s = jax.nn.sigmoid(g)
            act = g * s
            hid[some, :] = (act * u).astype(BF16)
            gui[some, :] = (h * act).astype(BF16)
            ggi[some, :] = (h * u * s * (1.0 + g * (1.0 - s))).astype(BF16)
            return carry2

        lax.fori_loop(0, SR // 32, activate, 0)
        sa[part(0, 0, b), :] = nn(hid[rows, :], wd[later]).astype(BF16)
        sa[part(0, 1, b), :] = (nt(ggi[rows, :], wg[later]) + nt(gui[rows, :], wu[later])).astype(BF16)

        @pl.when(step == 0)
        def _():
            for d in range(2):
                relay_copy(0, d).start()

        for d in range(2):
            @pl.when(step == 1 + d)
            def _():
                final_copy(0, 1 - d, d).start()

        return carry

    lax.fori_loop(0, NY, middle, 0)
    load_weights(NC + 1)
    load_weights(NC + 2)
    accg[:, : 2 * TOK] = jnp.zeros((ROWS, 2 * TOK), F32)

    def drain_early(n, carry):
        for d in range(2):
            for kind in range(2):
                first_copy(n, kind, d).wait_send()
            first_pass(n, d).wait_send()
        return carry

    lax.fori_loop(0, NF, drain_early, 0)

    def send_back(q, base):
        out_rows = sa[pl.ds(STAGE, ROWS), :]
        dx_rows = sa[pl.ds(STAGE + ROWS, ROWS), :]
        for h in range(2):
            p = perm[:, h * 2 * SR : (h + 1) * 2 * SR]
            o = tn(p, out_rows).reshape(NE // 2, HB, CW)
            d = tn(p, dx_rows).reshape(NE // 2, HB, CW)
            both = jnp.concatenate([o, d], axis=1).reshape(FR // 2, CW)
            sa[pl.ds(mo(base + h * (FR // 2), BLK), FR // 2), :] = both.astype(BF16)
        mine = pl.ds(mo(e * FB, BLK), FB)
        backf[q, mine, :] = sa[pl.ds(mo(base + e * FB, BLK), FB), :]
        plane_send(base, backf.at[q, mine], bsend.at[q], brecv.at[q])

    def parts_step(j, carry):
        u = NC + j
        for w in weight_copies(u):
            w.wait()
        b = lax.rem(u, 2)
        plane_first = lax.rem(j, 2) == 0
        base = jnp.where(plane_first, part_base(j // 2), STAGE)

        def half(h, carry2):
            rows = pl.ds(mo(h * 2 * SR, 2 * SR), 2 * SR)
            at = base + h * 2 * SR
            sa[pl.ds(mo(at, BLK), 2 * SR), :] = nn(hid[rows, :], wd[b]).astype(BF16)
            dx = nt(ggi[rows, :], wg[b]) + nt(gui[rows, :], wu[b])
            sa[pl.ds(mo(at + ROWS, BLK), 2 * SR), :] = dx.astype(BF16)
            return carry2

        lax.fori_loop(0, 2, half, 0)

        @pl.when(u + 2 < 2 * NC)
        def _():
            load_weights(u + 2)

        @pl.when(plane_first)
        def _():
            l = j // 2
            for d in range(2):
                relay_copy(l, d).start()
            for d in range(2):
                final_copy(l, 1 - d, d).start()

        @pl.when(lax.rem(j, 2) == 1)
        def _():
            n = (j - 1) // 2
            wait_plane(asend.at[n])
            send_back(n, n * FR)
            add_relay(n)

        return carry

    lax.fori_loop(1, NC, parts_step, 0)
    add_relay(NL - 1)

    def to_plane(l):
        for d in range(2):
            for kind in range(2):
                final_copy(l, kind, d).wait_recv()
        for kind in range(2):
            own = sa[part(l, kind, y), :].astype(F32)
            total = own + vrec[l, 0, kind].astype(F32) + vrec[l, 1, kind].astype(F32)
            sa[pl.ds(mo(STAGE + kind * ROWS + l * SR, BLK), SR), :] = total.astype(BF16)

    def parts_sent(l):
        for d in range(2):
            for kind in range(2):
                final_copy(l, kind, d).wait_send()
            relay_copy(l, d).wait_send()

    def sum_tokens(q, k, store):
        wait_plane(brecv.at[q])
        tc = sa[pl.ds(mo(TB + q * TR + NY * TOK, TOK), NY * TOK), :]
        parts = (slice(0, ROWS // 2), slice(ROWS // 2, ROWS))

        def rows_of(h, kind):
            return halves(backf[q, h * (FR // 2) : (h + 1) * (FR // 2), :], NE // 2)[kind]

        for h, rows in enumerate(parts):
            prod = nn(sel[k, rows, :], tc) * rows_of(h, 0)
            z = prod[:, :TOK]
            for b in range(1, CW // TOK):
                z = z + prod[:, b * TOK : (b + 1) * TOK]
            accg[rows, k * TOK : (k + 1) * TOK] += z
        lo = [(pf[k, rows, 0:1] * rows_of(h, 0)).astype(BF16) for h, rows in enumerate(parts)]
        store(0, tn(sel[k, parts[0], :], lo[0]) + tn(sel[k, parts[1], :], lo[1]))
        gt = [rows_of(h, 1).astype(BF16) for h in range(2)]
        store(1, tn(sel[k, parts[0], :], gt[0]) + tn(sel[k, parts[1], :], gt[1]))

    def sum_first(n):
        wait_plane(bsend.at[n])

        def keep(kind, v):
            for g in range(NY):
                sa[fpart(n, kind, g), :] = v[g * TOK : (g + 1) * TOK].astype(BF16)

        sum_tokens(n, 0, keep)
        for d in range(2):
            relay_first(n, d).start()
        for d in range(2):
            final_first(n, 1 - d, d).start()

    def drain_gathered(c, carry):
        for d in range(2):
            for kind in range(2):
                own_copy(c, kind, d).wait_send()
            pass_copy(c, d).wait_send()
        return carry

    lax.fori_loop(NF, NC, drain_gathered, 0)

    def scatter_step(i, carry):
        @pl.when((lax.rem(i, 2) == 1) & (i < 6))
        def _():
            sum_first((i - 1) // 2)

        @pl.when((lax.rem(i, 2) == 0) & (i >= 2))
        def _():
            n = i // 2 - 1
            for d in range(2):
                relay_first(n, d).wait_recv()
                rows = fpart(n, d, sides[d])
                sa[rows, :] = (sa[rows, :].astype(F32) + relayf[n, d].astype(F32)).astype(BF16)
                final_first(n, d, d).start()

        @pl.when(i < NL)
        def _():
            to_plane(i)

        @pl.when(i == NL - 1)
        def _():
            parts_sent(0)
            send_back(NF, PB)

        base = i * (2 * ROWS)
        xr = gath[pl.ds(mo(base, BLK), ROWS), :]
        cr = gath[pl.ds(mo(base + ROWS, BLK), ROWS), :]
        grads = [tn(xr, ggi[...]).astype(BF16), tn(xr, gui[...]).astype(BF16), tn(hid[...], cr).astype(BF16)]
        for k, v in enumerate(grads):
            gath[pl.ds(mo(base + k * CW, BLK), CW), :] = v
        return carry

    lax.fori_loop(0, NC, scatter_step, 0)

    def score_copies():
        return [
            pltpu.make_async_remote_copy(
                zbuf.at[3], zbuf.at[t], zsend.at[t], zrecv.at[t],
                device_id=((right, left, across)[t], e), device_id_type=MESH,
            )
            for t in range(3)
        ]

    ones = jnp.ones((8, TOK), BF16)
    z0, z1, z2 = split3(accg[:, :TOK])
    zbuf[3] = nt(ones, z0) + nt(ones, z1) + nt(ones, z2)
    for c in score_copies():
        c.start()

    def last_first(n, carry):
        for d in range(2):
            for kind in range(2):
                final_first(n, kind, d).wait_recv()
        for kind in range(2):
            own = sa[fpart(n, kind, y), :].astype(F32)
            total = own + vrecf[n, 0, kind].astype(F32) + vrecf[n, 1, kind].astype(F32)
            res[kind, n] = total.astype(BF16)
        return carry

    lax.fori_loop(0, NF, last_first, 0)

    def keep_last(kind, v):
        for l in range(NL):
            res[kind, NF + l] = v[l * TOK : (l + 1) * TOK].astype(BF16)

    sum_tokens(NF, 1, keep_last)

    for c in score_copies():
        c.wait_recv()
    zrow = (zbuf[3] + zbuf[0]) + (zbuf[1] + zbuf[2])
    group = lax.broadcasted_iota(jnp.int32, (NE, ROWS), 1) - HB * lax.broadcasted_iota(jnp.int32, (NE, ROWS), 0)
    group = (group >= 0) & (group < HB)
    z0, z1, z2 = split3(jnp.where(group, jnp.broadcast_to(zrow[0:1], (NE, ROWS)), 0.0))
    mine = sel[0, :, pl.ds(mo(y * TOK, TOK), TOK)]
    score = nn(z0, mine) + nn(z1, mine) + nn(z2, mine)
    z0, z1, z2 = split3(accg[:, TOK : 2 * TOK])
    zrow = nt(ones, z0) + nt(ones, z1) + nt(ones, z2)
    z0, z1, z2 = split3(jnp.where(group, jnp.broadcast_to(zrow[0:1], (NE, ROWS)), 0.0))
    for l in range(NL):
        mine = sel[1, :, l * TOK : (l + 1) * TOK]
        score = score + (nn(z0, mine) + nn(z1, mine) + nn(z2, mine))
    for k in range(TOP):
        gp_out[k : k + 1, :] = jnp.sum(jnp.where(ids[k : k + 1, :] == esub, score, 0.0), axis=0, keepdims=True)

    def drain(l, carry):
        parts_sent(l)
        return carry

    lax.fori_loop(1, NL, drain, 0)
    wait_plane(bsend.at[NF])

    def drain_first(n, carry):
        for d in range(2):
            for kind in range(2):
                final_first(n, kind, d).wait_send()
            relay_first(n, d).wait_send()
        return carry

    lax.fori_loop(0, NF, drain_first, 0)
    for c in table_copies() + score_copies():
        c.wait_send()

def keep_kernel(res, gp, grads, lo_out, gt_out, gp_out, gg_out, gu_out, gd_out, sem):
    gp_out[...] = gp[...]
    copies = []
    for c in range(NC):
        cols = pl.ds(c * CW, CW)
        pairs = [
            (grads.at[pl.ds((3 * c + k) * CW, CW)], out)
            for k, out in enumerate((gg_out.at[cols], gu_out.at[cols], gd_out.at[:, cols]))
        ]
        pairs += [(res.at[k, c], out.at[:, cols]) for k, out in enumerate((lo_out, gt_out))]
        copies += [pltpu.make_async_copy(src, dst, sem.at[k, c]) for k, (src, dst) in enumerate(pairs)]
    for c in copies:
        c.start()
    for c in copies:
        c.wait()


def keep(res, gp, grads):
    vm = pl.BlockSpec(memory_space=pltpu.VMEM)
    hbm = pl.BlockSpec(memory_space=pl.ANY)
    return pl.pallas_call(
        keep_kernel,
        out_shape=(
            jax.ShapeDtypeStruct((TOK, D), BF16),
            jax.ShapeDtypeStruct((TOK, D), BF16),
            jax.ShapeDtypeStruct((TOP, TOK), F32),
            jax.ShapeDtypeStruct((D, FF), BF16),
            jax.ShapeDtypeStruct((D, FF), BF16),
            jax.ShapeDtypeStruct((FF, D), BF16),
        ),
        in_specs=[hbm, vm, hbm],
        out_specs=(hbm, hbm, vm, hbm, hbm, hbm),
        scratch_shapes=[pltpu.SemaphoreType.DMA((5, NC))],
        compiler_params=pltpu.CompilerParams(vmem_limit_bytes=8 * 2**20),
    )(res, gp, grads)


def on_device(tokens, gate_probs, expert_ids, cotangent, w_gate, w_up, w_down):
    vm = pl.BlockSpec(memory_space=pltpu.VMEM)
    hbm = pl.BlockSpec(memory_space=pl.ANY)
    dma = pltpu.SemaphoreType.DMA
    flops = 9 * 2 * ROWS * D * FF
    res, gp, grads = pl.pallas_call(
        kernel,
        out_shape=(
            pltpu.VMEM((2, NC, TOK, CW), BF16),
            pltpu.VMEM((TOP, TOK), F32),
            pltpu.VMEM((NC * 2 * ROWS, CW), BF16),
        ),
        in_specs=[hbm] * 7,
        out_specs=(vm, vm, vm),
        scratch_shapes=[
            pltpu.VMEM((SA_ROWS, CW), BF16),
            pltpu.VMEM((2, CW, FF), BF16),
            pltpu.VMEM((2, CW, FF), BF16),
            pltpu.VMEM((2, FF, CW), BF16),
            pltpu.VMEM((ROWS, FF), F32),
            pltpu.VMEM((ROWS, FF), F32),
            pltpu.VMEM((ROWS, FF), F32),
            pltpu.VMEM((ROWS, FF), BF16),
            pltpu.VMEM((ROWS, FF), BF16),
            pltpu.VMEM((ROWS, FF), BF16),
            pltpu.VMEM((NL, 2, SR, CW), BF16),
            pltpu.VMEM((NL, 2, 2, SR, CW), BF16),
            pltpu.VMEM((NF, 2, TOK, CW), BF16),
            pltpu.VMEM((NF, 2, 2, TOK, CW), BF16),
            pltpu.VMEM((NX, FR, CW), BF16),
            pltpu.VMEM((2, ROWS, NY * TOK), BF16),
            pltpu.VMEM((2, ROWS, TOK), F32),
            pltpu.VMEM((ROWS, ROWS), BF16),
            pltpu.VMEM((NY, TOP, TOK), jnp.int32),
            pltpu.VMEM((NY, TOP, TOK), F32),
            pltpu.VMEM((4, 8, ROWS), F32),
            pltpu.VMEM((TOP, TOK), F32),
            pltpu.VMEM((TOP, TOK), jnp.int32),
            dma((3, 2)), dma((NX,)), dma((NX,)),
            dma((2, 3, NC)), dma((2, 3, NC)), dma((2, 3, NC)), dma((2, 3, NC)),
            dma((NX,)), dma((NX,)),
            dma((2, 3)), dma((2, 3)), dma((3,)), dma((3,)), dma((2, NC)), dma((2,)),
        ],
        compiler_params=pltpu.CompilerParams(
            collective_id=0, has_side_effects=True, vmem_limit_bytes=int(51.25 * 2**20)
        ),
        cost_estimate=pl.CostEstimate(flops=flops, bytes_accessed=37 * 2**20, transcendentals=ROWS * FF),
    )(tokens, gate_probs.T, expert_ids.T, cotangent, w_gate[0], w_up[0], w_down[0])
    lo, gt, gp, gg, gu, gd = keep(res, gp, grads)
    return lo, gt, gp.T, gg[None], gu[None], gd[None]


def solution(mesh):
    rows = P(("dp", "expert"), None)
    wide = P("expert", None, "dp")
    tall = P("expert", "dp", None)
    return jax.shard_map(
        on_device,
        mesh=mesh,
        in_specs=(rows, rows, rows, rows, wide, wide, tall),
        out_specs=(rows, rows, rows, wide, wide, tall),
        check_vma=False,
    )
```

```python
import jax
import jax.numpy as jnp
from jax import lax
from jax.experimental import pallas as pl
from jax.experimental.pallas import tpu as pltpu
from jax.sharding import PartitionSpec as P

MESH = pl.DeviceIdType.MESH
F32 = jnp.float32
BF16 = jnp.bfloat16

D = 3584
FF = 512
TOK = 128
TOP = 8
CAP = 6
NE = 32
NY = 4
NC = 7
CW = D // NC
NF = 3
NL = NC - NF
BLK = 16
FB = 48
HB = FB // 2
NX = NF + 1
FR = NE * FB
SR = NE * CAP
ROWS = NY * SR
TR = 2 * NY * TOK
AF = NX * FR
TB = 2 * NX * FR
SA_ROWS = TB + NX * TR
PB = NF * FR
STAGE = PB + NL * FR


def mo(v, m):
    return pl.multiple_of(v, m)


def nn(a, b):
    return lax.dot_general(a, b, (((1,), (0,)), ((), ())), preferred_element_type=F32)


def nt(a, b):
    return lax.dot_general(a, b, (((1,), (1,)), ((), ())), preferred_element_type=F32)


def tn(a, b):
    return lax.dot_general(a, b, (((0,), (0,)), ((), ())), preferred_element_type=F32)


def columns(c):
    return pl.ds(mo(c * CW, CW), CW)


def split3(v):
    a = v.astype(BF16)
    r = v - a.astype(F32)
    b = r.astype(BF16)
    return a, b, (r - b.astype(F32)).astype(BF16)


def kernel(
    tok_hbm, probs_hbm, ids_hbm, cot_hbm, wg_hbm, wu_hbm, wd_hbm,
    res, gp_out, gath,
    sa, wg, wu, wd, accg, accu, acch, hid, ggi, gui,
    relay, vrec, relayf, vrecf, backf,
    sel, pf, perm, idy, pry, zbuf, probs, ids,
    wsem, asend, arecv, ysend, yrecv, rsend, rrecv, bsend, brecv, tsend, trecv, zsend, zrecv, isem, tabsem,
):
    y = lax.axis_index("dp")
    e = lax.axis_index("expert")

    def trow(q, kind, g):
        return pl.ds(mo(TB + q * TR + kind * (NY * TOK) + g * TOK, TOK), TOK)

    def input_copies(c):
        q, g = jnp.minimum(c, NF), jnp.where(c < NF, y, c - NF)
        return (
            pltpu.make_async_copy(tok_hbm.at[:, columns(c)], sa.at[trow(q, 0, g)], isem.at[0, c]),
            pltpu.make_async_copy(cot_hbm.at[:, columns(c)], sa.at[trow(q, 1, g)], isem.at[1, c]),
        )

    def start_inputs(c, carry):
        for v in input_copies(c):
            v.start()
        return carry

    def wait_inputs(c, carry):
        for v in input_copies(c):
            v.wait()
        return carry

    lax.fori_loop(0, NC, start_inputs, 0)
    tables = (
        pltpu.make_async_copy(probs_hbm, probs, tabsem.at[0]),
        pltpu.make_async_copy(ids_hbm, ids, tabsem.at[1]),
    )
    for v in tables:
        v.start()
    right, left, across = lax.rem(y + 1, NY), lax.rem(y + 3, NY), lax.rem(y + 2, NY)
    sides = (right, left)
    ex, ez, ec = e // 8, lax.rem(e // 2, 4), lax.rem(e, 2)

    def peer(j):
        jx, jz, jc = lax.rem(j, 4), lax.rem(j // 4 + j, 4), j // 16
        return lax.rem(ex + jx, 4) * 8 + lax.rem(ez + jz, 4) * 2 + lax.rem(ec + jc, 2)

    barrier = pltpu.get_barrier_semaphore()
    for other in (right, left, across):
        pl.semaphore_signal(barrier, inc=1, device_id=(other, e), device_id_type=MESH)

    by_x = [lax.rem(ex + j, 4) * 8 for j in range(4)]
    by_z = [lax.rem(ez + j, 4) * 2 for j in range(4)]
    for j in range(1, NE):
        t = by_x[j % 4] + by_z[j // 4 % 4] + (ec if j < 16 else 1 - ec)
        pl.semaphore_signal(barrier, inc=1, device_id=(y, t), device_id_type=MESH)

    def chunk_of(u):
        out = jnp.where(u < 2, u, jnp.where(u == 6, 2, u + 1))
        j = u - NC
        home = jnp.where(lax.rem(j, 2) == 0, NF + j // 2, (j - 1) // 2)
        return jnp.where(u < NC, out, home)

    def weight_copies(u):
        cols = columns(chunk_of(u))
        b = lax.rem(u, 2)
        return (
            pltpu.make_async_copy(wg_hbm.at[cols], wg.at[b], wsem.at[0, b]),
            pltpu.make_async_copy(wu_hbm.at[cols], wu.at[b], wsem.at[1, b]),
            pltpu.make_async_copy(wd_hbm.at[:, cols], wd.at[b], wsem.at[2, b]),
        )

    def load_weights(u):
        for c in weight_copies(u):
            c.start()

    load_weights(0)
    load_weights(1)

    def first_copy(n, kind, d):
        return pltpu.make_async_remote_copy(
            sa.at[trow(n, kind, y)], sa.at[trow(n, kind, y)],
            ysend.at[d, kind, n], yrecv.at[d, kind, n], device_id=(sides[d], e), device_id_type=MESH,
        )

    def first_pass(n, d):
        ref = sa.at[trow(n, d, (left, right)[d])]
        return pltpu.make_async_remote_copy(
            ref, ref, ysend.at[d, 2, n], yrecv.at[d, 2, n], device_id=(sides[d], e), device_id_type=MESH,
        )

    def table_copies():
        return [
            pltpu.make_async_remote_copy(
                src, dst.at[y], tsend.at[k, t], trecv.at[k, t],
                device_id=((right, left, across)[t], e), device_id_type=MESH,
            )
            for t in range(3)
            for k, (src, dst) in enumerate(((ids, idy), (probs, pry)))
        ]

    def start_first(n, carry):
        for kind in range(2):
            for d in range(2):
                first_copy(n, kind, d).start()
        return carry

    lax.fori_loop(0, NC, wait_inputs, 0)
    for v in tables:
        v.wait()
    pl.semaphore_wait(barrier, NE + 2)
    lax.fori_loop(0, NF, start_first, 0)
    for c in table_copies():
        c.start()

    esub = lax.broadcasted_iota(jnp.int32, (NE, TOK), 0)
    lane = lax.broadcasted_iota(jnp.int32, (TOK, TOK), 1)
    sub = lax.broadcasted_iota(jnp.int32, (TOK, TOK), 0)
    before = jnp.where(sub < lane, 1.0, 0.0).astype(BF16)

    def routing(ids_v, probs_v):
        named = jnp.zeros((NE, TOK), F32)
        weight = jnp.zeros((NE, TOK), F32)
        for k in range(TOP):
            hit = ids_v[k : k + 1, :] == esub
            named = named + jnp.where(hit, 1.0, 0.0)
            weight = weight + jnp.where(hit, probs_v[k : k + 1, :], 0.0)
        rank = nn(named.astype(BF16), before)
        return jnp.where(named > 0.5, rank, 255.0), weight

    def spread_rows(v, count):
        return jnp.broadcast_to(v[:, None, :], (NE, count, TOK)).reshape(NE * count, TOK)

    fr_i = lax.rem(lax.broadcasted_iota(jnp.int32, (ROWS, TOK), 0), HB)

    def place(k, tables):
        p_rows = jnp.zeros((ROWS, 1), F32)
        for g, (code_g, weight_g) in enumerate(tables):
            here = (fr_i >= g * CAP) & (fr_i < (g + 1) * CAP)
            one = jnp.where(here & (spread_rows(code_g, HB) == (fr_i - g * CAP).astype(F32)), 1.0, 0.0)
            sel[k, :, g * TOK : (g + 1) * TOK] = one.astype(BF16)
            p_rows = p_rows + jnp.sum(one * spread_rows(weight_g, HB), axis=1, keepdims=True)
        pf[k] = jnp.broadcast_to(p_rows, (ROWS, TOK))

    own_table = routing(ids[...], probs[...])

    place(1, [own_table] * NL)

    def plane_send(base, arrival, send_sem, recv_sem):
        def send(j, carry):
            t = peer(j)
            pltpu.make_async_remote_copy(
                sa.at[pl.ds(mo(base + t * FB, BLK), FB)], arrival, send_sem, recv_sem,
                device_id=(y, t), device_id_type=MESH,
            ).start()
            return carry

        lax.fori_loop(1, NE, send, 0)

    def wait_plane(sem):
        blocks = sa.at[pl.ds(0, (NE - 1) * FB)]
        pltpu.make_async_copy(blocks, blocks, sem).wait()

    def build(q, k):
        mine = pl.ds(mo(AF + q * FR + e * FB, BLK), FB)
        base = q * FR
        tx = sa[pl.ds(mo(TB + q * TR, TOK), NY * TOK), :]
        tc = sa[pl.ds(mo(TB + q * TR + NY * TOK, TOK), NY * TOK), :]

        def quarter(i, carry2):
            rows = pl.ds(mo(i * SR, SR), SR)
            xr = nn(sel[k, rows, :], tx).reshape(8, HB, CW)
            cr = (pf[k, rows, 0:1] * nn(sel[k, rows, :], tc)).reshape(8, HB, CW)
            both = jnp.concatenate([xr, cr], axis=1).reshape(8 * FB, CW)
            sa[pl.ds(mo(base + i * (8 * FB), BLK), 8 * FB), :] = both.astype(BF16)
            return carry2

        lax.fori_loop(0, 4, quarter, 0)
        sa[mine, :] = sa[pl.ds(mo(base + e * FB, BLK), FB), :]
        plane_send(base, sa.at[mine], asend.at[q], arecv.at[q])

    build(NF, 1)

    r_i = lax.broadcasted_iota(jnp.int32, (ROWS, TOK), 0)
    q_i = lax.broadcasted_iota(jnp.int32, (ROWS, TOK), 1)
    y_i = r_i // SR
    r_i = r_i - y_i * SR
    src_i = r_i // CAP
    target = src_i * HB + y_i * CAP + (r_i - src_i * CAP)
    for b in range(ROWS // TOK):
        perm[:, b * TOK : (b + 1) * TOK] = jnp.where(q_i + b * TOK == target, 1.0, 0.0).astype(BF16)
    accg[...] = jnp.zeros((ROWS, FF), F32)
    accu[...] = jnp.zeros((ROWS, FF), F32)
    acch[...] = jnp.zeros((ROWS, FF), F32)

    def grow(c, kind, b):
        return pl.ds(mo(c * (2 * ROWS) + kind * ROWS + b * SR, BLK), SR)

    def gpair(c, kind, h):
        return pl.ds(mo(c * (2 * ROWS) + kind * ROWS + h * 2 * SR, BLK), 2 * SR)

    def own_copy(c, kind, d):
        ref = gath.at[grow(c, kind, y)]
        return pltpu.make_async_remote_copy(
            ref, ref, ysend.at[d, kind, c], yrecv.at[d, kind, c], device_id=(sides[d], e), device_id_type=MESH,
        )

    def pass_copy(c, d):
        ref = gath.at[grow(c, d, (left, right)[d])]
        return pltpu.make_async_remote_copy(
            ref, ref, ysend.at[d, 2, c], yrecv.at[d, 2, c], device_id=(sides[d], e), device_id_type=MESH,
        )

    def early(i, carry):
        for d in range(2):
            first_copy(i, d, d).wait_recv()
            first_pass(i, d).start()
        for d in range(2):
            first_copy(i, 1 - d, d).wait_recv()
        return carry

    lax.fori_loop(0, NF, early, 0)

    for c in table_copies():
        c.wait_recv()
    idy[y] = ids[...]
    pry[y] = probs[...]
    place(0, [routing(idy[g], pry[g]) for g in range(NY)])

    def halves(ref_rows, count):
        v = ref_rows.astype(F32).reshape(count, FB, CW)
        return v[:, :HB].reshape(count * HB, CW), v[:, HB:].reshape(count * HB, CW)

    def arrived(q, store):
        wait_plane(arecv.at[q])
        xs, cs = [], []
        for h in range(2):
            a, b = halves(sa[pl.ds(mo(AF + q * FR + h * (FR // 2), BLK), FR // 2), :], NE // 2)
            xs.append(a.astype(BF16))
            cs.append(b.astype(BF16))
        for kind, pieces in enumerate((xs, cs)):
            for h in range(2):
                p = perm[h * 2 * SR : (h + 1) * 2 * SR, :]
                rows = nn(p[:, : 2 * SR], pieces[0]) + nn(p[:, 2 * SR :], pieces[1])
                store(kind, h, rows.astype(BF16))

    def keep_plane(kind, h, rows):
        for i in range(2):
            gath[grow(NF + 2 * h + i, kind, y), :] = rows[i * SR : (i + 1) * SR]

    arrived(NF, keep_plane)
    for c in range(NF, NC):
        for kind in range(2):
            for d in range(2):
                own_copy(c, kind, d).start()

    def build_first(n, carry):
        for d in range(2):
            first_pass(n, d).wait_recv()
        build(n, 0)
        return carry

    lax.fori_loop(0, NF, build_first, 0)

    def gather_step(u, carry):
        c = chunk_of(u)

        @pl.when(u < 2)
        def _():
            for h in range(2):
                l = NF + 2 * u + h
                for d in range(2):
                    own_copy(l, d, d).wait_recv()
                    pass_copy(l, d).start()
                for d in range(2):
                    own_copy(l, 1 - d, d).wait_recv()

        @pl.when(u < 2)
        def _():
            def keep_first(kind, h, rows):
                gath[gpair(c, kind, h), :] = rows

            arrived(c, keep_first)

        @pl.when(u >= 2)
        def _():
            for d in range(2):
                pass_copy(c, d).wait_recv()

        for w in weight_copies(u):
            w.wait()
        b = lax.rem(u, 2)

        def half(h, carry2):
            rows = pl.ds(mo(h * 2 * SR, 2 * SR), 2 * SR)
            xr = gath[gpair(c, 0, h), :]
            cr = gath[gpair(c, 1, h), :]
            accg[rows, :] += nn(xr, wg[b])
            accu[rows, :] += nn(xr, wu[b])
            acch[rows, :] += nt(cr, wd[b])
            return carry2

        lax.fori_loop(0, 2, half, 0)
        @pl.when(u + 2 <= NC)
        def _():
            load_weights(u + 2)

        return carry

    lax.fori_loop(0, NC - 1, gather_step, 0)

    def keep_last_first(kind, h, rows):
        gath[gpair(NF - 1, kind, h), :] = rows

    arrived(NF - 1, keep_last_first)
    for u in (NC - 1, NC):
        for w in weight_copies(u):
            w.wait()
    wait_plane(asend.at[NF])
    now, later = (NC - 1) % 2, NC % 2

    def part_base(l):
        return PB + l * FR

    def part(l, kind, b):
        return pl.ds(mo(part_base(l) + kind * ROWS + b * SR, BLK), SR)

    def relay_copy(l, d):
        c = NF + l
        return pltpu.make_async_remote_copy(
            sa.at[part(l, d, across)], relay.at[l, d], rsend.at[d, 2, c], rrecv.at[d, 2, c],
            device_id=(sides[d], e), device_id_type=MESH,
        )

    def final_copy(l, kind, d):
        c = NF + l
        return pltpu.make_async_remote_copy(
            sa.at[part(l, kind, sides[d])], vrec.at[l, d, kind], rsend.at[d, kind, c], rrecv.at[d, kind, c],
            device_id=(sides[d], e), device_id_type=MESH,
        )

    def fpart(n, kind, b):
        return pl.ds(mo(n * FR + b * (2 * TOK) + kind * TOK, TOK), TOK)

    def relay_first(n, d):
        return pltpu.make_async_remote_copy(
            sa.at[fpart(n, d, across)], relayf.at[n, d], rsend.at[d, 2, n], rrecv.at[d, 2, n],
            device_id=(sides[d], e), device_id_type=MESH,
        )

    def final_first(n, kind, d):
        return pltpu.make_async_remote_copy(
            sa.at[fpart(n, kind, sides[d])], vrecf.at[n, d, kind], rsend.at[d, kind, n], rrecv.at[d, kind, n],
            device_id=(sides[d], e), device_id_type=MESH,
        )

    def add_relay(l):
        for d in range(2):
            relay_copy(l, d).wait_recv()
            rows = part(l, d, sides[d])
            sa[rows, :] = (sa[rows, :].astype(F32) + relay[l, d].astype(F32)).astype(BF16)
            final_copy(l, d, d).start()

    def middle(step, carry):
        b = lax.rem(y + jnp.where(step == 0, 2, jnp.where(step == 2, 3, jnp.where(step == 3, 0, 1))), NY)
        rows = pl.ds(mo(b * SR, SR), SR)
        xr, cr = gath[grow(NF - 1, 0, b), :], gath[grow(NF - 1, 1, b), :]
        accg[rows, :] += nn(xr, wg[now])
        accu[rows, :] += nn(xr, wu[now])
        acch[rows, :] += nt(cr, wd[now])

        def activate(i, carry2):
            some = pl.ds(mo(b * SR + i * 32, 32), 32)
            g, u, h = accg[some, :], accu[some, :], acch[some, :]
            s = jax.nn.sigmoid(g)
            act = g * s
            hid[some, :] = (act * u).astype(BF16)
            gui[some, :] = (h * act).astype(BF16)
            ggi[some, :] = (h * u * s * (1.0 + g * (1.0 - s))).astype(BF16)
            return carry2

        lax.fori_loop(0, SR // 32, activate, 0)
        sa[part(0, 0, b), :] = nn(hid[rows, :], wd[later]).astype(BF16)
        sa[part(0, 1, b), :] = (nt(ggi[rows, :], wg[later]) + nt(gui[rows, :], wu[later])).astype(BF16)

        @pl.when(step == 0)
        def _():
            for d in range(2):
                relay_copy(0, d).start()

        for d in range(2):
            @pl.when(step == 1 + d)
            def _():
                final_copy(0, 1 - d, d).start()

        return carry

    lax.fori_loop(0, NY, middle, 0)
    load_weights(NC + 1)
    load_weights(NC + 2)
    accg[:, : 2 * TOK] = jnp.zeros((ROWS, 2 * TOK), F32)

    def drain_early(n, carry):
        for d in range(2):
            for kind in range(2):
                first_copy(n, kind, d).wait_send()
            first_pass(n, d).wait_send()
        return carry

    lax.fori_loop(0, NF, drain_early, 0)

    def send_back(q, base):
        out_rows = sa[pl.ds(STAGE, ROWS), :]
        dx_rows = sa[pl.ds(STAGE + ROWS, ROWS), :]
        for h in range(2):
            p = perm[:, h * 2 * SR : (h + 1) * 2 * SR]
            o = tn(p, out_rows).reshape(NE // 2, HB, CW)
            d = tn(p, dx_rows).reshape(NE // 2, HB, CW)
            both = jnp.concatenate([o, d], axis=1).reshape(FR // 2, CW)
            sa[pl.ds(mo(base + h * (FR // 2), BLK), FR // 2), :] = both.astype(BF16)
        mine = pl.ds(mo(e * FB, BLK), FB)
        backf[q, mine, :] = sa[pl.ds(mo(base + e * FB, BLK), FB), :]
        plane_send(base, backf.at[q, mine], bsend.at[q], brecv.at[q])

    def parts_step(j, carry):
        u = NC + j
        for w in weight_copies(u):
            w.wait()
        b = lax.rem(u, 2)
        plane_first = lax.rem(j, 2) == 0
        base = jnp.where(plane_first, part_base(j // 2), STAGE)

        def half(h, carry2):
            rows = pl.ds(mo(h * 2 * SR, 2 * SR), 2 * SR)
            at = base + h * 2 * SR
            sa[pl.ds(mo(at, BLK), 2 * SR), :] = nn(hid[rows, :], wd[b]).astype(BF16)
            dx = nt(ggi[rows, :], wg[b]) + nt(gui[rows, :], wu[b])
            sa[pl.ds(mo(at + ROWS, BLK), 2 * SR), :] = dx.astype(BF16)
            return carry2

        lax.fori_loop(0, 2, half, 0)

        @pl.when(u + 2 < 2 * NC)
        def _():
            load_weights(u + 2)

        @pl.when(plane_first)
        def _():
            l = j // 2
            for d in range(2):
                relay_copy(l, d).start()
            for d in range(2):
                final_copy(l, 1 - d, d).start()

        @pl.when(lax.rem(j, 2) == 1)
        def _():
            n = (j - 1) // 2
            wait_plane(asend.at[n])
            send_back(n, n * FR)
            add_relay(n)

        return carry

    lax.fori_loop(1, NC, parts_step, 0)
    add_relay(NL - 1)

    def to_plane(l):
        for d in range(2):
            for kind in range(2):
                final_copy(l, kind, d).wait_recv()
        for kind in range(2):
            own = sa[part(l, kind, y), :].astype(F32)
            total = own + vrec[l, 0, kind].astype(F32) + vrec[l, 1, kind].astype(F32)
            sa[pl.ds(mo(STAGE + kind * ROWS + l * SR, BLK), SR), :] = total.astype(BF16)

    def parts_sent(l):
        for d in range(2):
            for kind in range(2):
                final_copy(l, kind, d).wait_send()
            relay_copy(l, d).wait_send()

    def sum_tokens(q, k, store):
        wait_plane(brecv.at[q])
        tc = sa[pl.ds(mo(TB + q * TR + NY * TOK, TOK), NY * TOK), :]
        parts = (slice(0, ROWS // 2), slice(ROWS // 2, ROWS))

        def rows_of(h, kind):
            return halves(backf[q, h * (FR // 2) : (h + 1) * (FR // 2), :], NE // 2)[kind]

        for h, rows in enumerate(parts):
            prod = (accu[rows, :] if k else nn(sel[k, rows, :], tc)) * rows_of(h, 0)
            z = prod[:, :TOK]
            for b in range(1, CW // TOK):
                z = z + prod[:, b * TOK : (b + 1) * TOK]
            accg[rows, k * TOK : (k + 1) * TOK] += z
        lo = [(pf[k, rows, 0:1] * rows_of(h, 0)).astype(BF16) for h, rows in enumerate(parts)]
        store(0, tn(sel[k, parts[0], :], lo[0]) + tn(sel[k, parts[1], :], lo[1]))
        gt = [rows_of(h, 1).astype(BF16) for h in range(2)]
        store(1, tn(sel[k, parts[0], :], gt[0]) + tn(sel[k, parts[1], :], gt[1]))

    def sum_first(n):
        wait_plane(bsend.at[n])

        def keep(kind, v):
            for g in range(NY):
                sa[fpart(n, kind, g), :] = v[g * TOK : (g + 1) * TOK].astype(BF16)

        sum_tokens(n, 0, keep)
        for d in range(2):
            relay_first(n, d).start()
        for d in range(2):
            final_first(n, 1 - d, d).start()

    def drain_gathered(c, carry):
        for d in range(2):
            for kind in range(2):
                own_copy(c, kind, d).wait_send()
            pass_copy(c, d).wait_send()
        return carry

    lax.fori_loop(NF, NC, drain_gathered, 0)

    def scatter_step(i, carry):
        @pl.when((lax.rem(i, 2) == 1) & (i < 6))
        def _():
            sum_first((i - 1) // 2)

        @pl.when((lax.rem(i, 2) == 0) & (i >= 2))
        def _():
            n = i // 2 - 1
            for d in range(2):
                relay_first(n, d).wait_recv()
                rows = fpart(n, d, sides[d])
                sa[rows, :] = (sa[rows, :].astype(F32) + relayf[n, d].astype(F32)).astype(BF16)
                final_first(n, d, d).start()

        @pl.when(i < NL)
        def _():
            to_plane(i)

        @pl.when(i == NL - 1)
        def _():
            parts_sent(0)
            send_back(NF, PB)

        base = i * (2 * ROWS)
        xr = gath[pl.ds(mo(base, BLK), ROWS), :]
        cr = gath[pl.ds(mo(base + ROWS, BLK), ROWS), :]
        grads = [tn(xr, ggi[...]).astype(BF16), tn(xr, gui[...]).astype(BF16), tn(hid[...], cr).astype(BF16)]
        for k, v in enumerate(grads):
            gath[pl.ds(mo(base + k * CW, BLK), CW), :] = v
        return carry

    lax.fori_loop(0, NC, scatter_step, 0)

    def score_copies():
        return [
            pltpu.make_async_remote_copy(
                zbuf.at[3], zbuf.at[t], zsend.at[t], zrecv.at[t],
                device_id=((right, left, across)[t], e), device_id_type=MESH,
            )
            for t in range(3)
        ]

    ones = jnp.ones((8, TOK), BF16)
    z0, z1, z2 = split3(accg[:, :TOK])
    zbuf[3] = nt(ones, z0) + nt(ones, z1) + nt(ones, z2)
    for c in score_copies():
        c.start()

    for h in range(2):
        last_c = sa[pl.ds(mo(TB + NF * TR + NY * TOK, TOK), NY * TOK), :]
        accu[h * 2 * SR : (h + 1) * 2 * SR, :] = nn(sel[1, h * 2 * SR : (h + 1) * 2 * SR, :], last_c)

    def last_first(n, carry):
        for d in range(2):
            for kind in range(2):
                final_first(n, kind, d).wait_recv()
        for kind in range(2):
            own = sa[fpart(n, kind, y), :].astype(F32)
            total = own + vrecf[n, 0, kind].astype(F32) + vrecf[n, 1, kind].astype(F32)
            res[kind, n] = total.astype(BF16)
        return carry

    lax.fori_loop(0, NF, last_first, 0)

    for c in score_copies():
        c.wait_recv()
    zrow = (zbuf[3] + zbuf[0]) + (zbuf[1] + zbuf[2])
    group = lax.broadcasted_iota(jnp.int32, (NE, ROWS), 1) - HB * lax.broadcasted_iota(jnp.int32, (NE, ROWS), 0)
    group = (group >= 0) & (group < HB)
    z0, z1, z2 = split3(jnp.where(group, jnp.broadcast_to(zrow[0:1], (NE, ROWS)), 0.0))
    mine = sel[0, :, pl.ds(mo(y * TOK, TOK), TOK)]
    score = nn(z0, mine) + nn(z1, mine) + nn(z2, mine)

    def keep_last(kind, v):
        for l in range(NL):
            res[kind, NF + l] = v[l * TOK : (l + 1) * TOK].astype(BF16)

    sum_tokens(NF, 1, keep_last)

    z0, z1, z2 = split3(accg[:, TOK : 2 * TOK])
    zrow = nt(ones, z0) + nt(ones, z1) + nt(ones, z2)
    z0, z1, z2 = split3(jnp.where(group, jnp.broadcast_to(zrow[0:1], (NE, ROWS)), 0.0))
    for l in range(NL):
        mine = sel[1, :, l * TOK : (l + 1) * TOK]
        score = score + (nn(z0, mine) + nn(z1, mine) + nn(z2, mine))
    for k in range(TOP):
        gp_out[k : k + 1, :] = jnp.sum(jnp.where(ids[k : k + 1, :] == esub, score, 0.0), axis=0, keepdims=True)

    def drain(l, carry):
        parts_sent(l)
        return carry

    lax.fori_loop(1, NL, drain, 0)
    wait_plane(bsend.at[NF])

    def drain_first(n, carry):
        for d in range(2):
            for kind in range(2):
                final_first(n, kind, d).wait_send()
            relay_first(n, d).wait_send()
        return carry

    lax.fori_loop(0, NF, drain_first, 0)
    for c in table_copies() + score_copies():
        c.wait_send()

def keep_kernel(res, gp, grads, lo_out, gt_out, gp_out, gg_out, gu_out, gd_out, sem):
    gp_out[...] = gp[...]
    copies = []
    for c in range(NC):
        cols = pl.ds(c * CW, CW)
        pairs = [
            (grads.at[pl.ds((3 * c + k) * CW, CW)], out)
            for k, out in enumerate((gg_out.at[cols], gu_out.at[cols], gd_out.at[:, cols]))
        ]
        pairs += [(res.at[k, c], out.at[:, cols]) for k, out in enumerate((lo_out, gt_out))]
        copies += [pltpu.make_async_copy(src, dst, sem.at[k, c]) for k, (src, dst) in enumerate(pairs)]
    for c in copies:
        c.start()
    for c in copies:
        c.wait()


def keep(res, gp, grads):
    vm = pl.BlockSpec(memory_space=pltpu.VMEM)
    hbm = pl.BlockSpec(memory_space=pl.ANY)
    return pl.pallas_call(
        keep_kernel,
        out_shape=(
            jax.ShapeDtypeStruct((TOK, D), BF16),
            jax.ShapeDtypeStruct((TOK, D), BF16),
            jax.ShapeDtypeStruct((TOP, TOK), F32),
            jax.ShapeDtypeStruct((D, FF), BF16),
            jax.ShapeDtypeStruct((D, FF), BF16),
            jax.ShapeDtypeStruct((FF, D), BF16),
        ),
        in_specs=[hbm, vm, hbm],
        out_specs=(hbm, hbm, vm, hbm, hbm, hbm),
        scratch_shapes=[pltpu.SemaphoreType.DMA((5, NC))],
        compiler_params=pltpu.CompilerParams(vmem_limit_bytes=8 * 2**20),
    )(res, gp, grads)


def on_device(tokens, gate_probs, expert_ids, cotangent, w_gate, w_up, w_down):
    vm = pl.BlockSpec(memory_space=pltpu.VMEM)
    hbm = pl.BlockSpec(memory_space=pl.ANY)
    dma = pltpu.SemaphoreType.DMA
    flops = 9 * 2 * ROWS * D * FF
    res, gp, grads = pl.pallas_call(
        kernel,
        out_shape=(
            pltpu.VMEM((2, NC, TOK, CW), BF16),
            pltpu.VMEM((TOP, TOK), F32),
            pltpu.VMEM((NC * 2 * ROWS, CW), BF16),
        ),
        in_specs=[hbm] * 7,
        out_specs=(vm, vm, vm),
        scratch_shapes=[
            pltpu.VMEM((SA_ROWS, CW), BF16),
            pltpu.VMEM((2, CW, FF), BF16),
            pltpu.VMEM((2, CW, FF), BF16),
            pltpu.VMEM((2, FF, CW), BF16),
            pltpu.VMEM((ROWS, FF), F32),
            pltpu.VMEM((ROWS, FF), F32),
            pltpu.VMEM((ROWS, FF), F32),
            pltpu.VMEM((ROWS, FF), BF16),
            pltpu.VMEM((ROWS, FF), BF16),
            pltpu.VMEM((ROWS, FF), BF16),
            pltpu.VMEM((NL, 2, SR, CW), BF16),
            pltpu.VMEM((NL, 2, 2, SR, CW), BF16),
            pltpu.VMEM((NF, 2, TOK, CW), BF16),
            pltpu.VMEM((NF, 2, 2, TOK, CW), BF16),
            pltpu.VMEM((NX, FR, CW), BF16),
            pltpu.VMEM((2, ROWS, NY * TOK), BF16),
            pltpu.VMEM((2, ROWS, TOK), F32),
            pltpu.VMEM((ROWS, ROWS), BF16),
            pltpu.VMEM((NY, TOP, TOK), jnp.int32),
            pltpu.VMEM((NY, TOP, TOK), F32),
            pltpu.VMEM((4, 8, ROWS), F32),
            pltpu.VMEM((TOP, TOK), F32),
            pltpu.VMEM((TOP, TOK), jnp.int32),
            dma((3, 2)), dma((NX,)), dma((NX,)),
            dma((2, 3, NC)), dma((2, 3, NC)), dma((2, 3, NC)), dma((2, 3, NC)),
            dma((NX,)), dma((NX,)),
            dma((2, 3)), dma((2, 3)), dma((3,)), dma((3,)), dma((2, NC)), dma((2,)),
        ],
        compiler_params=pltpu.CompilerParams(
            collective_id=0, has_side_effects=True, vmem_limit_bytes=int(51.25 * 2**20)
        ),
        cost_estimate=pl.CostEstimate(flops=flops, bytes_accessed=37 * 2**20, transcendentals=ROWS * FF),
    )(tokens, gate_probs.T, expert_ids.T, cotangent, w_gate[0], w_up[0], w_down[0])
    lo, gt, gp, gg, gu, gd = keep(res, gp, grads)
    return lo, gt, gp.T, gg[None], gu[None], gd[None]


def solution(mesh):
    rows = P(("dp", "expert"), None)
    wide = P("expert", None, "dp")
    tall = P("expert", "dp", None)
    return jax.shard_map(
        on_device,
        mesh=mesh,
        in_specs=(rows, rows, rows, rows, wide, wide, tall),
        out_specs=(rows, rows, rows, wide, wide, tall),
        check_vma=False,
    )
```
